32 devices in a mesh: space: 8 (over y, x, core), var: 4 (over z).
Axes of the slice: x: 2, y: 2, z: 4, core: 2. Of those that a mesh axis runs over, the one named last changes fastest.
Arguments:
- var_tokens: bfloat16 [16, 1024, 1024], P('var', 'space'), may hold values from -6 to 6
- key_query: bfloat16 [1024, 16], replicated
- value_weight: bfloat16 [1024, 1024], replicated, may hold values from -0.1875 to 0.1875
- qkv_weight: bfloat16 [1024, 3, 1024], P(None, None, 'var')
- out_weight: bfloat16 [1024, 1024], P('var'), may hold values from -0.1875 to 0.1875
- up_weight: bfloat16 [1024, 4096], P(None, 'var'), may hold values from -0.1875 to 0.1875
- down_weight: bfloat16 [4096, 1024], P('var'), may hold values from -0.09375 to 0.09375
- norm_gain: bfloat16 [1024], replicated, may hold values from 0.25 to 1.75
Outputs:
- block_out: bfloat16 [1024, 1024], P(('space', 'var'))
The draws below stay inside these ranges and needn't reach their ends.
All inputs are finite; a program needn't handle non-finite values.
Results may differ from the reference program's by a relative error of at most 0.018.
Values may be sent and summed in bfloat16 or wider, within the bound.
No kernel may reach another device: no remote copies, remote signals or barrier semaphores. Data moves between devices by JAX's collectives and lax.ppermute only.
A program may use at most 64 MiB of HBM per device.

```python
import math
import jax
import jax.numpy as jnp
from jax import lax

D = 1024
H = 16
FF = 4096
HD = 64
VARS = 16
TOKENS = 1024


def draw_key_query(key, part):
    base = jax.random.normal(key, (D, H), jnp.float32) * (2.0 / math.sqrt(D))
    return base.astype(jnp.bfloat16)


def draw_qkv_weight(key, part):
    inv_root = 1.0 / math.sqrt(D)
    base_key = jax.random.fold_in(key, 11)
    widen = jnp.array([1.6, 1.6, 1.0], jnp.float32)
    result = jnp.clip(jax.random.normal(base_key, (D, 3, D), jnp.float32), -4.0, 4.0) * inv_root
    result = result * widen[None, :, None]
    return result.astype(jnp.bfloat16)


def steps_of(stream_key, dims, shards, low, high):
    def one(axis_at, parts):
        draws = jax.random.uniform(jax.random.fold_in(jax.random.fold_in(stream_key, 6), axis_at), (parts,), jnp.float32, low / len(shards), high / len(shards))
        return jnp.repeat(jnp.exp(draws), dims[axis_at] // parts).reshape((-1,) + (1,) * (len(dims) - axis_at - 1))

    loudness = one(*shards[0])
    for cut in shards[1:]:
        loudness = loudness * one(*cut)
    return loudness


def centred(own_key, extent, deviation, bound, split=(), kind=jnp.bfloat16):
    values = deviation * jax.random.normal(own_key, extent, jnp.float32)
    if split:
        values = values * steps_of(own_key, extent, split, -0.22, 0.18)
    return jnp.clip(values, -bound, bound).astype(kind)


def setup_inputs(seed: int = 0) -> dict:
    seeds = jax.random.split(jax.random.key(seed), 9)
    var_tokens = centred(seeds[0], (VARS, TOKENS, D), 1.0, 6.0, ((0, 4), (1, 8)))
    key_query = draw_key_query(jax.random.fold_in(seeds[8], 71), 0)
    value_weight = centred(seeds[2], (D, D), D ** -0.5, 0.1875)
    qkv_weight = draw_qkv_weight(jax.random.fold_in(seeds[8], 71), 0)
    out_weight = centred(seeds[4], (D, D), D ** -0.5, 0.1875, ((0, 4),))
    up_weight = centred(seeds[5], (D, FF), D ** -0.5, 0.1875, ((1, 4),))
    down_weight = centred(seeds[6], (FF, D), FF ** -0.5, 0.09375, ((0, 4),))
    norm_gain = jnp.clip(1.0 + 0.15 * jax.random.normal(seeds[7], (D,), jnp.float32), 0.25, 1.75).astype(jnp.bfloat16)
    return dict(var_tokens=var_tokens, key_query=key_query, value_weight=value_weight, qkv_weight=qkv_weight, out_weight=out_weight, up_weight=up_weight, down_weight=down_weight, norm_gain=norm_gain)


def reference(var_tokens, key_query, value_weight, qkv_weight, out_weight, up_weight, down_weight, norm_gain):
    f32 = jnp.float32
    bf16 = jnp.bfloat16
    block_len = math.gcd(512, TOKENS)
    block_count = TOKENS // block_len

    def pool_block(block_index):
        first_row = (block_index * block_len).astype(jnp.int32)
        tokens_blk = lax.dynamic_slice_in_dim(var_tokens, first_row, block_len, 1).astype(f32)
        scores = jnp.einsum('vsd,dh->vsh', tokens_blk, key_query.astype(f32))
        values = jnp.einsum('vsd,de->vse', tokens_blk, value_weight.astype(f32)).astype(bf16)
        values = values.reshape(VARS, block_len, H, HD)
        top_score = lax.optimization_barrier(jnp.max(scores, axis=0))
        exp_terms = jnp.exp(scores - top_score[None])
        weight_sum = lax.optimization_barrier(jnp.sum(exp_terms, axis=0))
        numerator = jnp.einsum('vsh,vshe->she', exp_terms.astype(bf16).astype(f32), values.astype(f32))
        return (numerator / weight_sum[..., None]).reshape(block_len, D).astype(bf16)
    pooled = lax.map(pool_block, jnp.arange(block_count, dtype=jnp.int32)).reshape(TOKENS, D)
    pooled_f = pooled.astype(f32)
    mean_row = lax.optimization_barrier(jnp.mean(pooled_f, axis=1, keepdims=True))
    centered = pooled_f - mean_row
    spread = lax.optimization_barrier(jnp.mean(centered * centered, axis=1, keepdims=True))
    normed = (centered * lax.rsqrt(spread + 1e-05) * norm_gain.astype(f32)).astype(bf16)
    qkv = jnp.einsum('td,dcj->tcj', normed.astype(f32), qkv_weight.astype(f32)).astype(bf16)
    query_all = qkv[:, 0].reshape(TOKENS, H, HD).transpose(1, 0, 2)
    key_all = qkv[:, 1].reshape(TOKENS, H, HD).transpose(1, 0, 2)
    value_all = qkv[:, 2].reshape(TOKENS, H, HD).transpose(1, 0, 2)

    def one_head(operands):
        query_h, key_h, value_h = operands
        logits = jnp.dot(query_h, key_h.T, preferred_element_type=f32) * HD ** (-0.5)
        top_logit = lax.optimization_barrier(jnp.max(logits, axis=1, keepdims=True))
        exp_terms = jnp.exp(logits - top_logit)
        att_total = lax.optimization_barrier(jnp.sum(exp_terms, axis=1, keepdims=True))
        summed = jnp.dot(exp_terms.astype(bf16), value_h, preferred_element_type=f32)
        return (summed / att_total).astype(bf16)
    attended = lax.map(one_head, (query_all, key_all, value_all))
    attended = attended.transpose(1, 0, 2).reshape(TOKENS, D)
    hidden = jax.nn.gelu(jnp.dot(normed, up_weight, preferred_element_type=f32), approximate=True).astype(bf16)
    total_out = pooled_f + jnp.dot(attended, out_weight, preferred_element_type=f32) + jnp.dot(hidden, down_weight, preferred_element_type=f32)
    return total_out.astype(bf16)
```

```python
import functools

import jax
import jax.numpy as jnp
from jax import lax
from jax.experimental import pallas as pl
from jax.experimental.pallas import tpu as pltpu
from jax.sharding import PartitionSpec as P

H = 16
LANES = 128
EPS = 1e-05
f32 = jnp.float32
bf16 = jnp.bfloat16


def rows_of(refs):
    if len(refs) == 1:
        return refs[0][...]
    if refs[0].shape[0] % 16 == 0:
        return jnp.concatenate([r[...] for r in refs], axis=0)
    return jnp.concatenate([r[...].astype(f32) for r in refs], axis=0).astype(bf16)


def head_spread(first, last, width):
    lane = lax.broadcasted_iota(jnp.int32, (LANES, width), 0)
    column = lax.broadcasted_iota(jnp.int32, (LANES, width), 1)
    group = lane // H
    hit = (lane % H == column // (width // H)) & (group >= first) & (group < last)
    return hit.astype(bf16)


def split3(x):
    hi = x.astype(bf16).astype(f32)
    mid = (x - hi).astype(bf16).astype(f32)
    return hi, mid, x - hi - mid


def pool_kernel(me_ref, x_ref, kq_ref, wv_ref, *out_refs):
    n_vars, groups, rows, width = x_ref.shape
    me = me_ref[0]
    x = jnp.concatenate(
        [x_ref[v, me ^ k] for k in range(groups) for v in range(n_vars)], axis=0
    ) if rows % 16 == 0 else jnp.concatenate(
        [x_ref[v, me ^ k].astype(f32) for k in range(groups) for v in range(n_vars)], axis=0
    ).astype(bf16)
    kq = jnp.concatenate([kq_ref[...]] * (LANES // H), axis=0)
    scores = lax.dot_general(x, kq, (((1,), (1,)), ((), ())), preferred_element_type=f32)
    scores = scores.reshape(groups, n_vars, rows, LANES)
    top = jnp.max(scores, axis=1)
    terms = jnp.exp(scores - top[:, None])
    total = jnp.sum(terms, axis=1)
    share = (terms / total[:, None]).astype(bf16).reshape(groups * n_vars * rows, LANES)
    weights = jnp.dot(share, head_spread(0, 1, width), preferred_element_type=f32)
    values = jnp.dot(x, wv_ref[...], preferred_element_type=f32)
    mean = jnp.sum((weights * values).reshape(groups, n_vars, rows, width), axis=1)
    lane = lax.broadcasted_iota(jnp.int32, (rows, LANES), 1) // H
    for k in range(groups):
        stats = jnp.zeros((rows, LANES), f32)
        for j, part in enumerate(split3(top[k]) + split3(total[k])):
            stats = jnp.where(lane == j, part, stats)
        out_refs[k][:, :width] = mean[k].astype(bf16)
        out_refs[k][:, width:] = stats.astype(bf16)


def norm_kernel(gain_ref, *refs):
    parts, (normed_ref, pooled_ref) = refs[:-2], refs[-2:]
    rows, width = normed_ref.shape
    to_top = head_spread(0, 3, width)
    to_total = head_spread(3, 6, width)
    tops = [jnp.dot(p[:, width:], to_top, preferred_element_type=f32) for p in parts]
    totals = [jnp.dot(p[:, width:], to_total, preferred_element_type=f32) for p in parts]
    top = functools.reduce(jnp.maximum, tops)
    scales = [t * jnp.exp(m - top) for t, m in zip(totals, tops)]
    summed = functools.reduce(
        jnp.add, [s * p[:, :width].astype(f32) for s, p in zip(scales, parts)]
    )
    pooled = (summed / functools.reduce(jnp.add, scales)).astype(bf16)
    pooled_ref[...] = pooled
    pooled = pooled.astype(f32)
    centered = pooled - jnp.mean(pooled, axis=1, keepdims=True)
    spread = jnp.mean(centered * centered, axis=1, keepdims=True)
    normed_ref[...] = (centered * lax.rsqrt(spread + EPS) * gain_ref[...].astype(f32)).astype(bf16)


def qkv_kernel(w_ref, *refs):
    blocks, (q_ref, kv_ref) = refs[:-2], refs[-2:]
    x = rows_of(blocks)
    width = q_ref.shape[1]
    q_ref[...] = jnp.dot(x, w_ref[0], preferred_element_type=f32).astype(bf16)
    kv_ref[:, :width] = jnp.dot(x, w_ref[1], preferred_element_type=f32).astype(bf16)
    kv_ref[:, width:] = jnp.dot(x, w_ref[2], preferred_element_type=f32).astype(bf16)


def ffn_kernel(up_ref, down_ref, *refs):
    blocks, out_ref = refs[:-1], refs[-1]
    x = rows_of(blocks)
    hidden = jnp.dot(x, up_ref[...], preferred_element_type=f32)
    hidden = jax.nn.gelu(hidden, approximate=True).astype(bf16)
    out_ref[...] = jnp.dot(hidden, down_ref[...], preferred_element_type=f32)


def attend_kernel(heads, groups, q_ref, ffn_ref, wo_ref, *refs):
    blocks, out_refs = refs[:-groups], refs[-groups:]
    rows, width = q_ref.shape
    head_dim = width // heads
    q = q_ref[...].astype(f32) * head_dim ** (-0.5)
    owner = lax.broadcasted_iota(jnp.int32, (rows, width), 1) // head_dim
    stacked = jnp.concatenate([jnp.where(owner == h, q, 0.0) for h in range(heads)], axis=0)
    stacked = stacked.astype(bf16)
    keys = jnp.concatenate([b[:, :width] for b in blocks], axis=0)
    vals = jnp.concatenate([b[:, width:] for b in blocks], axis=0)
    logits = lax.dot_general(stacked, keys, (((1,), (1,)), ((), ())), preferred_element_type=f32)
    terms = jnp.exp(logits - jnp.max(logits, axis=1, keepdims=True))
    total = jnp.sum(terms, axis=1, keepdims=True)
    mixed = jnp.dot(terms.astype(bf16), vals, preferred_element_type=f32) / total
    attended = mixed[:rows]
    for h in range(1, heads):
        attended = jnp.where(owner == h, mixed[h * rows : (h + 1) * rows], attended)
    out = jnp.dot(attended.astype(bf16), wo_ref[...], preferred_element_type=f32) + ffn_ref[...]
    part = rows // groups
    for k in range(groups):
        out_refs[k][...] = out[k * part : (k + 1) * part].astype(bf16)


def add_kernel(*refs):
    out_ref = refs[-1]
    out_ref[...] = functools.reduce(jnp.add, [r[...].astype(f32) for r in refs[:-1]]).astype(bf16)


def call(kernel, out_shapes, *args, flops=0, smem=0, vmem=48):
    vmem_spec = pl.BlockSpec(memory_space=pltpu.VMEM)
    single = not isinstance(out_shapes, list)
    outs = [out_shapes] if single else out_shapes
    moved = sum(a.size * a.dtype.itemsize for a in (*args, *outs))
    result = pl.pallas_call(
        kernel,
        out_shape=outs,
        in_specs=[pl.BlockSpec(memory_space=pltpu.SMEM)] * smem + [vmem_spec] * (len(args) - smem),
        out_specs=[vmem_spec] * len(outs),
        compiler_params=pltpu.CompilerParams(vmem_limit_bytes=vmem << 20),
        cost_estimate=pl.CostEstimate(flops=flops, bytes_accessed=moved, transcendentals=0),
    )(*args)
    return result[0] if single else result


def exchange(parts, axis, size):
    return [parts[0]] + [
        lax.ppermute(parts[k], axis, [(i, i ^ k) for i in range(size)]) for k in range(1, size)
    ]


def gather_space(block, size):
    if size > 8:
        return [lax.all_gather(block, "space", axis=0, tiled=True)]
    blocks = exchange_chips(block, size)
    twin = [(i, i ^ 1) for i in range(size)]
    return blocks + [lax.ppermute(b, "space", twin) for b in blocks]


def exchange_chips(block, size):
    return [block] + [
        lax.ppermute(block, "space", [(i, i ^ k) for i in range(size)]) for k in range(2, size, 2)
    ]


def per_device(
    var_tokens, key_query, value_weight, qkv_weight, out_weight, up_weight, down_weight, norm_gain
):
    groups = lax.axis_size("var")
    spaces = lax.axis_size("space")
    n_vars, rows, width = var_tokens.shape
    part = rows // groups
    local = qkv_weight.shape[2]
    me = lax.axis_index("var").astype(jnp.int32).reshape(1)

    tokens = var_tokens.reshape(n_vars, groups, part, width)
    shape = jax.ShapeDtypeStruct
    sent = call(
        pool_kernel,
        [shape((part, width + LANES), bf16)] * groups,
        me, tokens, key_query.T, value_weight,
        flops=2 * n_vars * rows * width * width, smem=1,
    )
    got = exchange(sent, "var", groups)
    normed, pooled = call(
        norm_kernel, [shape((part, width), bf16)] * 2, norm_gain.reshape(1, width), *got
    )
    blocks = exchange([normed] * groups, "var", groups)
    q, kv = call(
        qkv_kernel,
        [shape((rows, local), bf16), shape((rows, 2 * local), bf16)],
        qkv_weight.transpose(1, 0, 2), *blocks,
        flops=6 * rows * width * local,
    )
    kv_blocks = gather_space(kv, spaces)
    hidden = up_weight.shape[1]
    ffn = call(
        ffn_kernel, shape((rows, width), f32), up_weight, down_weight, *blocks,
        flops=4 * rows * width * hidden,
    )
    sums = call(
        functools.partial(attend_kernel, H // groups, groups),
        [shape((part, width), bf16)] * groups,
        q, ffn, out_weight, *kv_blocks,
        flops=4 * rows * rows * spaces * local,
    )
    return call(add_kernel, shape((part, width), bf16), pooled, *exchange(sums, "var", groups))


def solution(mesh):
    placed = (
        P("var", "space", None),
        P(),
        P(),
        P(None, None, "var"),
        P("var", None),
        P(None, "var"),
        P("var", None),
        P(),
    )
    return jax.shard_map(
        per_device, mesh=mesh, in_specs=placed, out_specs=P(("space", "var"), None), check_vma=False
    )
```

```python
import functools
import math

import jax
import jax.numpy as jnp
from jax import lax
from jax.experimental import pallas as pl
from jax.experimental.pallas import tpu as pltpu
from jax.sharding import PartitionSpec as P

H = 16
LANES = 128
EPS = 1e-05
f32 = jnp.float32
bf16 = jnp.bfloat16


def rows_of(refs):
    return below([r[...] for r in refs])


def head_spread(first, last, width):
    lane = lax.broadcasted_iota(jnp.int32, (LANES, width), 0)
    column = lax.broadcasted_iota(jnp.int32, (LANES, width), 1)
    group = lane // H
    hit = (lane % H == column // (width // H)) & (group >= first) & (group < last)
    return hit.astype(bf16)


def split3(x):
    hi = x.astype(bf16).astype(f32)
    mid = (x - hi).astype(bf16).astype(f32)
    return hi, mid, x - hi - mid


def below(blocks):
    if blocks[0].shape[0] % 16 == 0:
        return jnp.concatenate(blocks, axis=0)
    return jnp.concatenate([b.astype(f32) for b in blocks], axis=0).astype(bf16)


def pool_kernel(batch, x_hbm, kq_hbm, wv_hbm, *refs):
    refs = refs[-len(batch) - 4 :]
    out_refs, (x_ref, kq_ref, wv_ref, sem) = refs[:-4], refs[-4:]
    me = lax.axis_index("var")
    copies = [pltpu.make_async_copy(kq_hbm, kq_ref, sem.at[0])]
    for i, k in enumerate(batch):
        copies.append(pltpu.make_async_copy(x_hbm.at[:, me ^ k], x_ref.at[i], sem.at[2 + i]))
    weights = pltpu.make_async_copy(wv_hbm, wv_ref, sem.at[1])
    for copy in (*copies, weights):
        copy.start()
    for copy in copies:
        copy.wait()
    slots, n_vars, rows, width = x_ref.shape
    x = below([x_ref[k, v] for k in range(slots) for v in range(n_vars)])
    kq = jnp.concatenate([kq_ref[...]] * (LANES // H), axis=0)
    scores = lax.dot_general(x, kq, (((1,), (1,)), ((), ())), preferred_element_type=f32)
    scores = scores.reshape(slots, n_vars, rows, LANES)
    top = jnp.max(scores, axis=1)
    terms = jnp.exp(scores - top[:, None])
    total = jnp.sum(terms, axis=1)
    share = (terms / total[:, None]).astype(bf16).reshape(slots * n_vars * rows, LANES)
    lane = lax.broadcasted_iota(jnp.int32, (rows, LANES), 1) // H
    for k in range(slots):
        stats = jnp.zeros((rows, LANES), f32)
        for j, part in enumerate(split3(top[k]) + split3(total[k])):
            stats = jnp.where(lane == j, part, stats)
        out_refs[k][:, width:] = stats.astype(bf16)
    share = jnp.dot(share, head_spread(0, 1, width), preferred_element_type=f32)
    weights.wait()
    values = jnp.dot(x, wv_ref[...], preferred_element_type=f32)
    mean = jnp.sum((share * values).reshape(slots, n_vars, rows, width), axis=1)
    for k in range(slots):
        out_refs[k][:, :width] = mean[k].astype(bf16)


def norm_kernel(gain_ref, *refs):
    parts, (normed_ref, pooled_ref) = refs[:-2], refs[-2:]
    rows, width = normed_ref.shape
    to_top = head_spread(0, 3, width)
    to_total = head_spread(3, 6, width)
    tops = [jnp.dot(p[:, width:], to_top, preferred_element_type=f32) for p in parts]
    totals = [jnp.dot(p[:, width:], to_total, preferred_element_type=f32) for p in parts]
    top = functools.reduce(jnp.maximum, tops)
    scales = [t * jnp.exp(m - top) for t, m in zip(totals, tops)]
    summed = functools.reduce(
        jnp.add, [s * p[:, :width].astype(f32) for s, p in zip(scales, parts)]
    )
    pooled = (summed / functools.reduce(jnp.add, scales)).astype(bf16)
    pooled_ref[...] = pooled
    pooled = pooled.astype(f32)
    centered = pooled - jnp.mean(pooled, axis=1, keepdims=True)
    spread = jnp.mean(centered * centered, axis=1, keepdims=True)
    normed_ref[...] = (centered * lax.rsqrt(spread + EPS) * gain_ref[...].astype(f32)).astype(bf16)


def qkv_kernel(w_ref, *refs):
    blocks, (q_ref, kv_ref) = refs[:-2], refs[-2:]
    x = rows_of(blocks)
    width = q_ref.shape[1]
    q_ref[...] = jnp.dot(x, w_ref[0], preferred_element_type=f32).astype(bf16)
    kv_ref[:, :width] = jnp.dot(x, w_ref[1], preferred_element_type=f32).astype(bf16)
    kv_ref[:, width:] = jnp.dot(x, w_ref[2], preferred_element_type=f32).astype(bf16)


def ffn_kernel(up_ref, down_ref, *refs):
    blocks, out_ref = refs[:-1], refs[-1]
    x = rows_of(blocks)
    hidden = jnp.dot(x, up_ref[...], preferred_element_type=f32)
    hidden = jax.nn.gelu(hidden, approximate=True).astype(bf16)
    out_ref[...] = jnp.dot(hidden, down_ref[...], preferred_element_type=f32)


def attend_kernel(heads, groups, q_ref, ffn_ref, wo_ref, *refs):
    blocks, out_refs = refs[:-groups], refs[-groups:]
    rows, width = q_ref.shape
    head_dim = width // heads
    q = q_ref[...].astype(f32) * head_dim ** (-0.5)
    owner = lax.broadcasted_iota(jnp.int32, (rows, width), 1) // head_dim
    stacked = jnp.concatenate([jnp.where(owner == h, q, 0.0) for h in range(heads)], axis=0)
    stacked = stacked.astype(bf16)
    keys = jnp.concatenate([b[:, :width] for b in blocks], axis=0)
    vals = jnp.concatenate([b[:, width:] for b in blocks], axis=0)
    logits = lax.dot_general(stacked, keys, (((1,), (1,)), ((), ())), preferred_element_type=f32)
    terms = jnp.exp(logits - jnp.max(logits, axis=1, keepdims=True))
    total = jnp.sum(terms, axis=1, keepdims=True)
    mixed = jnp.dot(terms.astype(bf16), vals, preferred_element_type=f32) / total
    attended = mixed[:rows]
    for h in range(1, heads):
        attended = jnp.where(owner == h, mixed[h * rows : (h + 1) * rows], attended)
    out = jnp.dot(attended.astype(bf16), wo_ref[...], preferred_element_type=f32) + ffn_ref[...]
    part = rows // groups
    for k in range(groups):
        out_refs[k][...] = out[k * part : (k + 1) * part].astype(bf16)


def add_kernel(*refs):
    out_ref = refs[-1]
    out_ref[...] = functools.reduce(jnp.add, [r[...].astype(f32) for r in refs[:-1]]).astype(bf16)


def call(kernel, out_shapes, *args, flops=0, vmem=16, hbm=0, scratch=()):
    spec = pl.BlockSpec(memory_space=pltpu.VMEM)
    moved = sum(math.prod(a.shape) * jnp.dtype(a.dtype).itemsize for a in (*args, *out_shapes))
    args = [
        pltpu.with_memory_space_constraint(a, pltpu.HBM if i < hbm else pltpu.VMEM)
        for i, a in enumerate(args)
    ]
    return pl.pallas_call(
        kernel,
        out_shape=out_shapes,
        in_specs=[pl.BlockSpec(memory_space=pltpu.HBM)] * hbm + [spec] * (len(args) - hbm),
        out_specs=[spec] * len(out_shapes),
        scratch_shapes=scratch,
        compiler_params=pltpu.CompilerParams(vmem_limit_bytes=vmem << 20),
        cost_estimate=pl.CostEstimate(flops=flops, bytes_accessed=moved, transcendentals=0),
    )(*args)


def exchange(parts, axis, size):
    got = [
        lax.ppermute(parts[k], axis, [(i, i ^ k) for i in range(size)])
        for k in reversed(range(1, size))
    ]
    return [*got, parts[0]]


def gather_space(block, size):
    if size > 8:
        return [lax.all_gather(block, "space", axis=0, tiled=True)]
    blocks = exchange_chips(block, size)
    twin = [(i, i ^ 1) for i in range(size)]
    return blocks + [lax.ppermute(b, "space", twin) for b in blocks]


def exchange_chips(block, size):
    return [block] + [
        lax.ppermute(block, "space", [(i, i ^ k) for i in range(size)])
        for k in reversed(range(2, size, 2))
    ]


def per_device(
    var_tokens, key_query, value_weight, qkv_weight, out_weight, up_weight, down_weight, norm_gain
):
    groups = lax.axis_size("var")
    spaces = lax.axis_size("space")
    n_vars, rows, width = var_tokens.shape
    part = rows // groups
    local = qkv_weight.shape[2]

    shape = pltpu.VMEM
    order = list(reversed(range(groups)))
    sent = []
    for batch in (order[: groups // 2], order[groups // 2 :]):
        sent += call(
            functools.partial(pool_kernel, batch),
            [shape((part, width + LANES), bf16)] * len(batch),
            var_tokens.reshape(n_vars, groups, part, width), key_query.T, value_weight, *sent[:1],
            flops=2 * n_vars * part * width * width * len(batch), hbm=3, vmem=24,
            scratch=[
                pltpu.VMEM((len(batch), n_vars, part, width), bf16),
                pltpu.VMEM((H, width), bf16),
                pltpu.VMEM((width, width), bf16),
                pltpu.SemaphoreType.DMA((2 + len(batch),)),
            ],
        )
    got = exchange(sent[::-1], "var", groups)
    normed, pooled = call(
        norm_kernel, [shape((part, width), bf16)] * 2, norm_gain.reshape(1, width), *got
    )
    blocks = exchange([normed] * groups, "var", groups)
    q, kv = call(
        qkv_kernel,
        [shape((rows, local), bf16), shape((rows, 2 * local), bf16)],
        qkv_weight.transpose(1, 0, 2), *blocks,
        flops=6 * rows * width * local,
    )
    kv_blocks = gather_space(kv, spaces)
    hidden = up_weight.shape[1]
    (ffn,) = call(
        ffn_kernel, [shape((rows, width), f32)], up_weight, down_weight, *blocks,
        flops=4 * rows * width * hidden,
    )
    sums = call(
        functools.partial(attend_kernel, H // groups, groups),
        [shape((part, width), bf16)] * groups,
        q, ffn, out_weight, *kv_blocks,
        flops=4 * rows * rows * spaces * local, vmem=32,
    )
    (out,) = call(add_kernel, [jax.ShapeDtypeStruct((part, width), bf16)], pooled, *exchange(sums[::-1], "var", groups))
    return out


def solution(mesh):
    placed = (
        P("var", "space", None),
        P(),
        P(),
        P(None, None, "var"),
        P("var", None),
        P(None, "var"),
        P("var", None),
        P(),
    )
    return jax.shard_map(
        per_device, mesh=mesh, in_specs=placed, out_specs=P(("space", "var"), None), check_vma=False
    )
```

```python
import functools
import math

import jax
import jax.numpy as jnp
from jax import lax
from jax.experimental import pallas as pl
from jax.experimental.pallas import tpu as pltpu
from jax.sharding import PartitionSpec as P

H = 16
LANES = 128
EPS = 1e-05
f32 = jnp.float32
bf16 = jnp.bfloat16


def rows_of(refs):
    return below([r[...] for r in refs])


def head_spread(first, last, width):
    lane = lax.broadcasted_iota(jnp.int32, (LANES, width), 0)
    column = lax.broadcasted_iota(jnp.int32, (LANES, width), 1)
    group = lane // H
    hit = (lane % H == column // (width // H)) & (group >= first) & (group < last)
    return hit.astype(bf16)


def split3(x):
    hi = x.astype(bf16).astype(f32)
    mid = (x - hi).astype(bf16).astype(f32)
    return hi, mid, x - hi - mid


def below(blocks):
    if blocks[0].shape[0] % 16 == 0:
        return jnp.concatenate(blocks, axis=0)
    return jnp.concatenate([b.astype(f32) for b in blocks], axis=0).astype(bf16)


def load_kernel(x_hbm, kq_hbm, wv_hbm, tokens_any, wv_any, share_ref, stats_ref, x_ref, kq_ref, sem):
    me = lax.axis_index("var")
    slots, n_vars, rows, _ = x_ref.shape
    copies = [pltpu.make_async_copy(kq_hbm, kq_ref, sem.at[0])]
    for k in range(slots):
        copies.append(pltpu.make_async_copy(x_hbm.at[:, me ^ k], x_ref.at[k], sem.at[3 + k]))
    weights = pltpu.make_async_copy(wv_hbm, wv_any, sem.at[1])
    for copy in (*copies, weights):
        copy.start()
    for copy in copies:
        copy.wait()
    passing = pltpu.make_async_copy(x_ref, tokens_any, sem.at[2])
    passing.start()
    x = below([x_ref[k, v] for k in range(slots) for v in range(n_vars)])
    kq = jnp.concatenate([kq_ref[...]] * (LANES // H), axis=0)
    scores = lax.dot_general(x, kq, (((1,), (1,)), ((), ())), preferred_element_type=f32)
    scores = scores.reshape(slots, n_vars, rows, LANES)
    top = jnp.max(scores, axis=1)
    terms = jnp.exp(scores - top[:, None])
    total = jnp.sum(terms, axis=1)
    share_ref[...] = (terms / total[:, None]).astype(bf16)
    lane = lax.broadcasted_iota(jnp.int32, top.shape, 2) // H
    stats = jnp.zeros(top.shape, f32)
    for j, part in enumerate(split3(top) + split3(total)):
        stats = jnp.where(lane == j, part, stats)
    stats_ref[...] = stats.astype(bf16)
    passing.wait()
    weights.wait()


def pool_kernel(slot, x_ref, wv_ref, share_ref, stats_ref, *refs):
    out_ref = refs[-1]
    n_vars, rows, width = x_ref.shape[1:]
    share = below([share_ref[slot, v] for v in range(n_vars)])
    share = jnp.dot(share, head_spread(0, 1, width), preferred_element_type=f32)
    x = below([x_ref[slot, v] for v in range(n_vars)])
    values = jnp.dot(x, wv_ref[...], preferred_element_type=f32)
    mean = jnp.sum((share * values).reshape(n_vars, rows, width), axis=0)
    out_ref[:, :width] = mean.astype(bf16)
    out_ref[:, width:] = stats_ref[slot]


def norm_kernel(gain_ref, *refs):
    parts, (normed_ref, pooled_ref) = refs[:-2], refs[-2:]
    rows, width = normed_ref.shape
    to_top = head_spread(0, 3, width)
    to_total = head_spread(3, 6, width)
    tops = [jnp.dot(p[:, width:], to_top, preferred_element_type=f32) for p in parts]
    totals = [jnp.dot(p[:, width:], to_total, preferred_element_type=f32) for p in parts]
    top = functools.reduce(jnp.maximum, tops)
    scales = [t * jnp.exp(m - top) for t, m in zip(totals, tops)]
    summed = functools.reduce(
        jnp.add, [s * p[:, :width].astype(f32) for s, p in zip(scales, parts)]
    )
    pooled = (summed / functools.reduce(jnp.add, scales)).astype(bf16)
    pooled_ref[...] = pooled
    pooled = pooled.astype(f32)
    centered = pooled - jnp.mean(pooled, axis=1, keepdims=True)
    spread = jnp.mean(centered * centered, axis=1, keepdims=True)
    normed_ref[...] = (centered * lax.rsqrt(spread + EPS) * gain_ref[...].astype(f32)).astype(bf16)


def qkv_kernel(w_ref, *refs):
    blocks, (q_ref, kv_ref) = refs[:-2], refs[-2:]
    x = rows_of(blocks)
    width = q_ref.shape[1]
    q_ref[...] = jnp.dot(x, w_ref[0], preferred_element_type=f32).astype(bf16)
    kv_ref[:, :width] = jnp.dot(x, w_ref[1], preferred_element_type=f32).astype(bf16)
    kv_ref[:, width:] = jnp.dot(x, w_ref[2], preferred_element_type=f32).astype(bf16)


def ffn_kernel(up_ref, down_ref, *refs):
    blocks, out_ref = refs[:-3], refs[-2]
    x = rows_of(blocks)
    hidden = jnp.dot(x, up_ref[...], preferred_element_type=f32)
    hidden = jax.nn.gelu(hidden, approximate=True).astype(bf16)
    out_ref[...] = jnp.dot(hidden, down_ref[...], preferred_element_type=f32)


def attend(heads, q_ref, blocks):
    rows, width = q_ref.shape
    head_dim = width // heads
    q = q_ref[...].astype(f32) * head_dim ** (-0.5)
    owner = lax.broadcasted_iota(jnp.int32, (rows, width), 1) // head_dim
    stacked = jnp.concatenate([jnp.where(owner == h, q, 0.0) for h in range(heads)], axis=0)
    stacked = stacked.astype(bf16)
    keys = jnp.concatenate([b[:, :width] for b in blocks], axis=0)
    vals = jnp.concatenate([b[:, width:] for b in blocks], axis=0)
    logits = lax.dot_general(stacked, keys, (((1,), (1,)), ((), ())), preferred_element_type=f32)
    top = jnp.max(logits, axis=1, keepdims=True)
    terms = jnp.exp(logits - top)
    total = jnp.sum(terms, axis=1, keepdims=True)
    mixed = jnp.dot(terms.astype(bf16), vals, preferred_element_type=f32)

    def own_head(stack):
        out = jnp.broadcast_to(stack[:rows], (rows, width))
        for h in range(1, heads):
            out = jnp.where(owner == h, stack[h * rows : (h + 1) * rows], out)
        return out

    return own_head(mixed), own_head(top), own_head(total)


def early_kernel(heads, q_ref, *refs):
    blocks, out_refs = refs[:-3], refs[-3:]
    for ref, value in zip(out_refs, attend(heads, q_ref, blocks)):
        ref[...] = value


def attend_kernel(heads, groups, q_ref, ffn_ref, wo_ref, mixed_ref, top_ref, total_ref, *refs):
    blocks, out_refs = refs[:-groups], refs[-groups:]
    mixed, top, total = attend(heads, q_ref, blocks)
    both = jnp.maximum(top, top_ref[...])
    late, early = jnp.exp(top - both), jnp.exp(top_ref[...] - both)
    attended = (mixed * late + mixed_ref[...] * early) / (total * late + total_ref[...] * early)
    out = jnp.dot(attended.astype(bf16), wo_ref[...], preferred_element_type=f32) + ffn_ref[...]
    part = out.shape[0] // groups
    for k in range(groups):
        out_refs[k][...] = out[k * part : (k + 1) * part].astype(bf16)


def add_kernel(*refs):
    out_ref = refs[-1]
    out_ref[...] = functools.reduce(jnp.add, [r[...].astype(f32) for r in refs[:-1]]).astype(bf16)


def call(kernel, out_shapes, *args, flops=0, vmem=16, hbm=0, scratch=(), any_outs=(), aliases={}):
    moved = sum(math.prod(a.shape) * jnp.dtype(a.dtype).itemsize for a in (*args, *out_shapes))
    args = [
        pltpu.with_memory_space_constraint(a, pltpu.HBM if i < hbm else pltpu.VMEM)
        for i, a in enumerate(args)
    ]
    in_specs = [pl.BlockSpec(memory_space=pltpu.HBM if i < hbm else pltpu.VMEM) for i in range(len(args))]
    out_specs = [pl.BlockSpec(memory_space=pltpu.VMEM)] * len(out_shapes)
    for i in any_outs:
        out_specs[i] = pl.BlockSpec(memory_space=pl.ANY)
    for i, o in aliases.items():
        in_specs[i] = out_specs[o] = pl.BlockSpec(memory_space=pl.ANY)
    return pl.pallas_call(
        kernel,
        out_shape=out_shapes,
        in_specs=in_specs,
        out_specs=out_specs,
        input_output_aliases=aliases,
        scratch_shapes=scratch,
        compiler_params=pltpu.CompilerParams(vmem_limit_bytes=vmem << 20),
        cost_estimate=pl.CostEstimate(flops=flops, bytes_accessed=moved, transcendentals=0),
    )(*args)


def exchange(parts, axis, size):
    got = [
        lax.ppermute(parts[k], axis, [(i, i ^ k) for i in range(size)])
        for k in reversed(range(1, size))
    ]
    return [*got, parts[0]]


def gather_space(block, size, between):
    if size > 8:
        blocks = between(lax.all_gather(block, "space", axis=0, tiled=True))
        half = blocks.shape[0] // 2
        return [blocks[:half]], [blocks[half:]]
    blocks = [block] + [
        lax.ppermute(block, "space", [(i, i ^ k) for i in range(size)]) for k in reversed(range(2, size, 2))
    ]
    blocks[1] = between(blocks[1])
    twin = [(i, i ^ 1) for i in range(size)]
    twins = [lax.ppermute(b, "space", twin) for b in blocks]
    return blocks + twins[:2], twins[2:]


def per_device(
    var_tokens, key_query, value_weight, qkv_weight, out_weight, up_weight, down_weight, norm_gain
):
    groups = lax.axis_size("var")
    spaces = lax.axis_size("space")
    n_vars, rows, width = var_tokens.shape
    part = rows // groups
    local = qkv_weight.shape[2]

    shape = pltpu.VMEM
    kept = (groups, n_vars, part)
    loaded = call(
        load_kernel,
        [
            shape((*kept, width), bf16),
            shape(value_weight.shape, bf16),
            shape((*kept, LANES), bf16),
            shape((groups, part, LANES), bf16),
        ],
        var_tokens.reshape(n_vars, groups, part, width), key_query.T, value_weight,
        flops=2 * n_vars * rows * width * LANES, hbm=3, any_outs=(0, 1),
        scratch=[
            pltpu.VMEM((*kept, width), bf16),
            pltpu.VMEM((H, width), bf16),
            pltpu.SemaphoreType.DMA((3 + groups,)),
        ],
    )
    sent = []
    for slot in reversed(range(groups)):
        sent += call(
            functools.partial(pool_kernel, slot), [shape((part, width + LANES), bf16)],
            *loaded, *sent[-1:],
            flops=2 * n_vars * part * width * width,
        )
    got = exchange(sent[::-1], "var", groups)
    normed, pooled = call(
        norm_kernel, [shape((part, width), bf16)] * 2, norm_gain.reshape(1, width), *got
    )
    blocks = exchange([normed] * groups, "var", groups)
    q, kv = call(
        qkv_kernel,
        [shape((rows, local), bf16), shape((rows, 2 * local), bf16)],
        qkv_weight.transpose(1, 0, 2), *blocks,
        flops=6 * rows * width * local,
    )
    ffn = []

    def feed_forward(arrived):
        made = call(
            ffn_kernel, [shape((rows, width), f32), shape(arrived.shape, bf16)],
            up_weight, down_weight, *blocks, arrived,
            flops=4 * rows * width * up_weight.shape[1], aliases={2 + len(blocks): 1},
        )
        ffn.append(made[0])
        return made[1]

    early, late = gather_space(kv, spaces, feed_forward)
    heads = H // groups
    state = call(
        functools.partial(early_kernel, heads), [shape((rows, local), f32)] * 3, q, *early,
        flops=4 * rows * rows * len(early) * local * heads, vmem=32,
    )
    sums = call(
        functools.partial(attend_kernel, heads, groups),
        [shape((part, width), bf16)] * groups,
        q, *ffn, out_weight, *state, *late,
        flops=4 * rows * rows * len(late) * local * heads, vmem=32,
    )
    (out,) = call(add_kernel, [jax.ShapeDtypeStruct((part, width), bf16)], pooled, *exchange(sums[::-1], "var", groups))
    return out


def solution(mesh):
    placed = (
        P("var", "space", None),
        P(),
        P(),
        P(None, None, "var"),
        P("var", None),
        P(None, "var"),
        P("var", None),
        P(),
    )
    return jax.shard_map(
        per_device, mesh=mesh, in_specs=placed, out_specs=P(("space", "var"), None), check_vma=False
    )
```

```python
import functools
import math

import jax
import jax.numpy as jnp
from jax import lax
from jax.experimental import pallas as pl
from jax.experimental.pallas import tpu as pltpu
from jax.sharding import PartitionSpec as P

H = 16
LANES = 128
EPS = 1e-05
f32 = jnp.float32
bf16 = jnp.bfloat16


def rows_of(refs):
    return below([r[...] for r in refs])


def head_spread(first, last, width):
    lane = lax.broadcasted_iota(jnp.int32, (LANES, width), 0)
    column = lax.broadcasted_iota(jnp.int32, (LANES, width), 1)
    group = lane // H
    hit = (lane % H == column // (width // H)) & (group >= first) & (group < last)
    return hit.astype(bf16)


def split3(x):
    hi = x.astype(bf16).astype(f32)
    mid = (x - hi).astype(bf16).astype(f32)
    return hi, mid, x - hi - mid


def below(blocks):
    if blocks[0].shape[0] % 16 == 0:
        return jnp.concatenate(blocks, axis=0)
    return jnp.concatenate([b.astype(f32) for b in blocks], axis=0).astype(bf16)


def load_kernel(x_hbm, kq_hbm, wv_hbm, tokens_any, wv_any, share_ref, stats_ref, x_ref, kq_ref, sem):
    me = lax.axis_index("var")
    slots, n_vars, rows, _ = x_ref.shape
    copies = [pltpu.make_async_copy(kq_hbm, kq_ref, sem.at[0])]
    for k in range(slots):
        copies.append(pltpu.make_async_copy(x_hbm.at[:, me ^ k], x_ref.at[k], sem.at[3 + k]))
    weights = pltpu.make_async_copy(wv_hbm, wv_any, sem.at[1])
    for copy in (*copies, weights):
        copy.start()
    for copy in copies:
        copy.wait()
    passing = pltpu.make_async_copy(x_ref, tokens_any, sem.at[2])
    passing.start()
    x = below([x_ref[k, v] for k in range(slots) for v in range(n_vars)])
    kq = jnp.concatenate([kq_ref[...]] * (LANES // H), axis=0)
    scores = lax.dot_general(x, kq, (((1,), (1,)), ((), ())), preferred_element_type=f32)
    scores = scores.reshape(slots, n_vars, rows, LANES)
    top = jnp.max(scores, axis=1)
    terms = jnp.exp(scores - top[:, None])
    total = jnp.sum(terms, axis=1)
    share_ref[...] = (terms / total[:, None]).astype(bf16)
    lane = lax.broadcasted_iota(jnp.int32, top.shape, 2) // H
    stats = jnp.zeros(top.shape, f32)
    for j, part in enumerate(split3(top) + split3(total)):
        stats = jnp.where(lane == j, part, stats)
    stats_ref[...] = stats.astype(bf16)
    passing.wait()
    weights.wait()


def pool_kernel(slot, x_ref, wv_ref, share_ref, stats_ref, out_ref):
    n_vars, rows, width = x_ref.shape[1:]
    share = below([share_ref[slot, v] for v in range(n_vars)])
    share = jnp.dot(share, head_spread(0, 1, width), preferred_element_type=f32)
    x = below([x_ref[slot, v] for v in range(n_vars)])
    values = jnp.dot(x, wv_ref[...], preferred_element_type=f32)
    mean = jnp.sum((share * values).reshape(n_vars, rows, width), axis=0)
    out_ref[:, :width] = mean.astype(bf16)
    out_ref[:, width:] = stats_ref[slot]


def norm_kernel(gain_ref, *refs):
    parts, (normed_ref, pooled_ref) = refs[:-2], refs[-2:]
    rows, width = normed_ref.shape
    to_top = head_spread(0, 3, width)
    to_total = head_spread(3, 6, width)
    tops = [jnp.dot(p[:, width:], to_top, preferred_element_type=f32) for p in parts]
    totals = [jnp.dot(p[:, width:], to_total, preferred_element_type=f32) for p in parts]
    top = functools.reduce(jnp.maximum, tops)
    scales = [t * jnp.exp(m - top) for t, m in zip(totals, tops)]
    summed = functools.reduce(
        jnp.add, [s * p[:, :width].astype(f32) for s, p in zip(scales, parts)]
    )
    pooled = (summed / functools.reduce(jnp.add, scales)).astype(bf16)
    pooled_ref[...] = pooled
    pooled = pooled.astype(f32)
    centered = pooled - jnp.mean(pooled, axis=1, keepdims=True)
    spread = jnp.mean(centered * centered, axis=1, keepdims=True)
    normed_ref[...] = (centered * lax.rsqrt(spread + EPS) * gain_ref[...].astype(f32)).astype(bf16)


def qkv_kernel(w_ref, *refs):
    blocks, (q_ref, kv_ref, kept_ref) = refs[:-3], refs[-3:]
    x = rows_of(blocks)
    width = q_ref.shape[1]
    q_ref[...] = jnp.dot(x, w_ref[0], preferred_element_type=f32).astype(bf16)
    kv_ref[:, :width] = jnp.dot(x, w_ref[1], preferred_element_type=f32).astype(bf16)
    kv_ref[:, width:] = jnp.dot(x, w_ref[2], preferred_element_type=f32).astype(bf16)
    kept_ref[...] = kv_ref[...]


def ffn_kernel(up_ref, down_ref, *refs):
    blocks, out_ref = refs[:-3], refs[-2]
    x = rows_of(blocks)
    hidden = jnp.dot(x, up_ref[...], preferred_element_type=f32)
    hidden = jax.nn.gelu(hidden, approximate=True).astype(bf16)
    out_ref[...] = jnp.dot(hidden, down_ref[...], preferred_element_type=f32)


def attend(heads, q_ref, blocks):
    rows, width = q_ref.shape
    head_dim = width // heads
    q = q_ref[...].astype(f32) * head_dim ** (-0.5)
    owner = lax.broadcasted_iota(jnp.int32, (rows, width), 1) // head_dim
    stacked = jnp.concatenate([jnp.where(owner == h, q, 0.0) for h in range(heads)], axis=0)
    stacked = stacked.astype(bf16)
    keys = jnp.concatenate([b[:, :width] for b in blocks], axis=0)
    vals = jnp.concatenate([b[:, width:] for b in blocks], axis=0)
    logits = lax.dot_general(stacked, keys, (((1,), (1,)), ((), ())), preferred_element_type=f32)
    top = jnp.max(logits, axis=1, keepdims=True)
    terms = jnp.exp(logits - top)
    total = jnp.sum(terms, axis=1, keepdims=True)
    mixed = jnp.dot(terms.astype(bf16), vals, preferred_element_type=f32)

    def own_head(stack):
        out = jnp.broadcast_to(stack[:rows], (rows, width))
        for h in range(1, heads):
            out = jnp.where(owner == h, stack[h * rows : (h + 1) * rows], out)
        return out

    return own_head(mixed), own_head(top), own_head(total)


def early_kernel(heads, q_ref, *refs):
    blocks, out_refs = refs[:-3], refs[-3:]
    for ref, value in zip(out_refs, attend(heads, q_ref, blocks)):
        ref[...] = value


def attend_kernel(heads, groups, q_ref, ffn_ref, wo_ref, mixed_ref, top_ref, total_ref, *refs):
    blocks, out_refs = refs[:-groups], refs[-groups:]
    mixed, top, total = attend(heads, q_ref, blocks)
    both = jnp.maximum(top, top_ref[...])
    late, early = jnp.exp(top - both), jnp.exp(top_ref[...] - both)
    attended = (mixed * late + mixed_ref[...] * early) / (total * late + total_ref[...] * early)
    out = jnp.dot(attended.astype(bf16), wo_ref[...], preferred_element_type=f32) + ffn_ref[...]
    part = out.shape[0] // groups
    for k in range(groups):
        out_refs[k][...] = out[k * part : (k + 1) * part].astype(bf16)


def add_kernel(*refs):
    out_ref = refs[-1]
    out_ref[...] = functools.reduce(jnp.add, [r[...].astype(f32) for r in refs[:-1]]).astype(bf16)


def call(kernel, out_shapes, *args, flops=0, vmem=16, hbm=0, scratch=(), any_outs=(), aliases={}):
    moved = sum(math.prod(a.shape) * jnp.dtype(a.dtype).itemsize for a in (*args, *out_shapes))
    args = [
        pltpu.with_memory_space_constraint(a, pltpu.HBM if i < hbm else pltpu.VMEM)
        for i, a in enumerate(args)
    ]
    in_specs = [pl.BlockSpec(memory_space=pltpu.HBM if i < hbm else pltpu.VMEM) for i in range(len(args))]
    out_specs = [pl.BlockSpec(memory_space=pltpu.VMEM)] * len(out_shapes)
    for i in any_outs:
        out_specs[i] = pl.BlockSpec(memory_space=pl.ANY)
    for i, o in aliases.items():
        in_specs[i] = out_specs[o] = pl.BlockSpec(memory_space=pl.ANY)
    return pl.pallas_call(
        kernel,
        out_shape=out_shapes,
        in_specs=in_specs,
        out_specs=out_specs,
        input_output_aliases=aliases,
        scratch_shapes=scratch,
        compiler_params=pltpu.CompilerParams(vmem_limit_bytes=vmem << 20),
        cost_estimate=pl.CostEstimate(flops=flops, bytes_accessed=moved, transcendentals=0),
    )(*args)


def exchange(parts, axis, size, partners):
    return [lax.ppermute(parts[k], axis, [(i, i ^ k) for i in range(size)]) for k in partners]


def gather_space(block, kept, size):
    if size > 8:
        blocks = lax.all_gather(block, "space", axis=0, tiled=True)
        half = blocks.shape[0] // 2
        return [blocks[:half]], [blocks[half:]]
    blocks = [kept, *exchange([block] * size, "space", size, range(size - 2, 0, -2))]
    twins = [twin for b in blocks for twin in exchange([b, b], "space", size, (1,))]
    return blocks + twins[:2], twins[2:]


def per_device(
    var_tokens, key_query, value_weight, qkv_weight, out_weight, up_weight, down_weight, norm_gain
):
    groups = lax.axis_size("var")
    spaces = lax.axis_size("space")
    n_vars, rows, width = var_tokens.shape
    part = rows // groups
    local = qkv_weight.shape[2]
    partners = [range(groups - 1, 0, -1)] * 3
    if groups == 4:
        partners = (3, 2, 1), (1, 3, 2), (2, 1, 3)

    shape = pltpu.VMEM
    kept = (groups, n_vars, part)
    loaded = call(
        load_kernel,
        [
            shape((*kept, width), bf16),
            shape(value_weight.shape, bf16),
            shape((*kept, LANES), bf16),
            shape((groups, part, LANES), bf16),
        ],
        var_tokens.reshape(n_vars, groups, part, width), key_query.T, value_weight,
        flops=2 * n_vars * rows * width * LANES, hbm=3, any_outs=(0, 1),
        scratch=[
            pltpu.VMEM((*kept, width), bf16),
            pltpu.VMEM((H, width), bf16),
            pltpu.SemaphoreType.DMA((3 + groups,)),
        ],
    )
    sent = []
    for slot in reversed(range(groups)):
        sent += call(
            functools.partial(pool_kernel, slot), [shape((part, width + LANES), bf16)],
            *loaded,
            flops=2 * n_vars * part * width * width,
        )
    got = exchange(sent[::-1], "var", groups, partners[0])
    normed, pooled = call(
        norm_kernel, [shape((part, width), bf16)] * 2, norm_gain.reshape(1, width), *got, sent[-1]
    )
    blocks = [*exchange([normed] * groups, "var", groups, partners[1]), normed]
    q, kv, kept = call(
        qkv_kernel,
        [shape((rows, local), bf16)] + [shape((rows, 2 * local), bf16)] * 2,
        qkv_weight.transpose(1, 0, 2), *blocks,
        flops=6 * rows * width * local,
    )
    ffn = []

    def feed_forward(arrived):
        made = call(
            ffn_kernel, [shape((rows, width), f32), shape(arrived.shape, bf16)],
            up_weight, down_weight, *blocks, arrived,
            flops=4 * rows * width * up_weight.shape[1], aliases={2 + len(blocks): 1},
        )
        ffn.append(made[0])
        return made[1]

    early, late = gather_space(kv, feed_forward(kept), spaces)
    heads = H // groups
    state = call(
        functools.partial(early_kernel, heads), [shape((rows, local), f32)] * 3, q, *early,
        flops=4 * rows * rows * len(early) * local * heads, vmem=32,
    )
    sums = call(
        functools.partial(attend_kernel, heads, groups),
        [shape((part, width), bf16)] * groups,
        q, *ffn, out_weight, *state, *late,
        flops=4 * rows * rows * len(late) * local * heads, vmem=32,
    )
    by_partner = dict(zip([*partners[1], 0], sums))
    got = exchange(by_partner, "var", groups, partners[2])
    (out,) = call(
        add_kernel, [jax.ShapeDtypeStruct((part, width), bf16)], pooled, *got, by_partner[0]
    )
    return out


def solution(mesh):
    placed = (
        P("var", "space", None),
        P(),
        P(),
        P(None, None, "var"),
        P("var", None),
        P(None, "var"),
        P("var", None),
        P(),
    )
    return jax.shard_map(
        per_device, mesh=mesh, in_specs=placed, out_specs=P(("space", "var"), None), check_vma=False
    )
```

```python
import functools
import math

import jax
import jax.numpy as jnp
from jax import lax
from jax.experimental import pallas as pl
from jax.experimental.pallas import tpu as pltpu
from jax.sharding import PartitionSpec as P

H = 16
LANES = 128
EPS = 1e-05
f32 = jnp.float32
bf16 = jnp.bfloat16


def rows_of(refs):
    return below([r[...] for r in refs])


def head_spread(first, last, width):
    lane = lax.broadcasted_iota(jnp.int32, (LANES, width), 0)
    column = lax.broadcasted_iota(jnp.int32, (LANES, width), 1)
    group = lane // H
    hit = (lane % H == column // (width // H)) & (group >= first) & (group < last)
    return hit.astype(bf16)


def split3(x):
    hi = x.astype(bf16).astype(f32)
    mid = (x - hi).astype(bf16).astype(f32)
    return hi, mid, x - hi - mid


def below(blocks):
    if blocks[0].shape[0] % 16 == 0:
        return jnp.concatenate(blocks, axis=0)
    return jnp.concatenate([b.astype(f32) for b in blocks], axis=0).astype(bf16)


def load_kernel(x_hbm, kq_hbm, wv_hbm, tokens_any, wv_any, share_ref, stats_ref, x_ref, kq_ref, sem):
    me = lax.axis_index("var")
    slots, n_vars, rows, _ = x_ref.shape
    copies = [pltpu.make_async_copy(kq_hbm, kq_ref, sem.at[0])]
    for k in range(slots):
        copies.append(pltpu.make_async_copy(x_hbm.at[:, me ^ k], x_ref.at[k], sem.at[3 + k]))
    weights = pltpu.make_async_copy(wv_hbm, wv_any, sem.at[1])
    for copy in (*copies, weights):
        copy.start()
    for copy in copies:
        copy.wait()
    passing = pltpu.make_async_copy(x_ref, tokens_any, sem.at[2])
    passing.start()
    x = below([x_ref[k, v] for k in range(slots) for v in range(n_vars)])
    kq = jnp.concatenate([kq_ref[...]] * (LANES // H), axis=0)
    scores = lax.dot_general(x, kq, (((1,), (1,)), ((), ())), preferred_element_type=f32)
    scores = scores.reshape(slots, n_vars, rows, LANES)
    top = jnp.max(scores, axis=1)
    terms = jnp.exp(scores - top[:, None])
    total = jnp.sum(terms, axis=1)
    share_ref[...] = (terms / total[:, None]).astype(bf16)
    lane = lax.broadcasted_iota(jnp.int32, top.shape, 2) // H
    stats = jnp.zeros(top.shape, f32)
    for j, part in enumerate(split3(top) + split3(total)):
        stats = jnp.where(lane == j, part, stats)
    stats_ref[...] = stats.astype(bf16)
    passing.wait()
    weights.wait()


def pool_kernel(slot, x_ref, wv_ref, share_ref, stats_ref, out_ref):
    n_vars, rows, width = x_ref.shape[1:]
    share = below([share_ref[slot, v] for v in range(n_vars)])
    share = jnp.dot(share, head_spread(0, 1, width), preferred_element_type=f32)
    x = below([x_ref[slot, v] for v in range(n_vars)])
    values = jnp.dot(x, wv_ref[...], preferred_element_type=f32)
    mean = jnp.sum((share * values).reshape(n_vars, rows, width), axis=0)
    out_ref[:, :width] = mean.astype(bf16)
    out_ref[:, width:] = stats_ref[slot]


def norm_kernel(gain_ref, *refs):
    parts, (normed_ref, pooled_ref) = refs[:-2], refs[-2:]
    rows, width = normed_ref.shape
    to_top = head_spread(0, 3, width)
    to_total = head_spread(3, 6, width)
    tops = [jnp.dot(p[:, width:], to_top, preferred_element_type=f32) for p in parts]
    totals = [jnp.dot(p[:, width:], to_total, preferred_element_type=f32) for p in parts]
    top = functools.reduce(jnp.maximum, tops)
    scales = [t * jnp.exp(m - top) for t, m in zip(totals, tops)]
    summed = functools.reduce(
        jnp.add, [s * p[:, :width].astype(f32) for s, p in zip(scales, parts)]
    )
    pooled = (summed / functools.reduce(jnp.add, scales)).astype(bf16)
    pooled_ref[...] = pooled
    pooled = pooled.astype(f32)
    centered = pooled - jnp.mean(pooled, axis=1, keepdims=True)
    spread = jnp.mean(centered * centered, axis=1, keepdims=True)
    normed_ref[...] = (centered * lax.rsqrt(spread + EPS) * gain_ref[...].astype(f32)).astype(bf16)


def qkv_kernel(w_ref, *refs):
    blocks, (q_ref, kv_ref, kept_ref) = refs[:-3], refs[-3:]
    x = rows_of(blocks)
    width = q_ref.shape[1]
    q_ref[...] = jnp.dot(x, w_ref[0], preferred_element_type=f32).astype(bf16)
    kv_ref[:, :width] = jnp.dot(x, w_ref[1], preferred_element_type=f32).astype(bf16)
    kv_ref[:, width:] = jnp.dot(x, w_ref[2], preferred_element_type=f32).astype(bf16)
    kept_ref[...] = kv_ref[...]


def ffn_kernel(up_ref, down_ref, *refs):
    blocks, out_ref = refs[:-3], refs[-2]
    x = rows_of(blocks)
    hidden = jnp.dot(x, up_ref[...], preferred_element_type=f32)
    hidden = jax.nn.gelu(hidden, approximate=True).astype(bf16)
    out_ref[...] = jnp.dot(hidden, down_ref[...], preferred_element_type=f32)


def attend(heads, q_ref, blocks, span):
    rows, width = q_ref.shape
    head_dim = width // heads
    span = min(width, span)
    owner = lax.broadcasted_iota(jnp.int32, (rows, span), 1) // head_dim
    together = span // head_dim
    results = []
    for first in range(0, width, span):
        own = slice(first, first + span)
        q = q_ref[:, own].astype(f32) * head_dim ** (-0.5)
        q = jnp.concatenate([jnp.where(owner == h, q, 0.0) for h in range(together)], axis=0)
        keys = jnp.concatenate([b[:, own] for b in blocks], axis=0)
        vals = jnp.concatenate([b[:, width + first : width + first + span] for b in blocks], axis=0)
        logits = lax.dot_general(
            q.astype(bf16), keys, (((1,), (1,)), ((), ())), preferred_element_type=f32
        )
        top = jnp.max(logits, axis=1, keepdims=True)
        terms = jnp.exp(logits - top)
        total = jnp.sum(terms, axis=1, keepdims=True)
        mixed = jnp.dot(terms.astype(bf16), vals, preferred_element_type=f32)
        for i, stack in enumerate((mixed, top, total)):
            out = jnp.broadcast_to(stack[:rows], (rows, span))
            for h in range(1, together):
                out = jnp.where(owner == h, stack[h * rows : (h + 1) * rows], out)
            results.append(out)
    return [jnp.concatenate(results[i::3], axis=1) for i in range(3)]


def early_kernel(heads, q_ref, *refs):
    blocks, out_refs = refs[:-3], refs[-3:]
    for ref, value in zip(out_refs, attend(heads, q_ref, blocks, LANES)):
        ref[...] = value


def attend_kernel(heads, groups, q_ref, ffn_ref, wo_ref, mixed_ref, top_ref, total_ref, *refs):
    blocks, out_refs = refs[:-groups], refs[-groups:]
    mixed, top, total = attend(heads, q_ref, blocks, q_ref.shape[1])
    both = jnp.maximum(top, top_ref[...])
    late, early = jnp.exp(top - both), jnp.exp(top_ref[...] - both)
    attended = (mixed * late + mixed_ref[...] * early) / (total * late + total_ref[...] * early)
    out = jnp.dot(attended.astype(bf16), wo_ref[...], preferred_element_type=f32) + ffn_ref[...]
    part = out.shape[0] // groups
    for k in range(groups):
        out_refs[k][...] = out[k * part : (k + 1) * part].astype(bf16)


def add_kernel(*refs):
    out_ref = refs[-1]
    out_ref[...] = functools.reduce(jnp.add, [r[...].astype(f32) for r in refs[:-1]]).astype(bf16)


def call(kernel, out_shapes, *args, flops=0, vmem=16, hbm=0, scratch=(), any_outs=(), aliases={}):
    moved = sum(math.prod(a.shape) * jnp.dtype(a.dtype).itemsize for a in (*args, *out_shapes))
    args = [
        pltpu.with_memory_space_constraint(a, pltpu.HBM if i < hbm else pltpu.VMEM)
        for i, a in enumerate(args)
    ]
    in_specs = [pl.BlockSpec(memory_space=pltpu.HBM if i < hbm else pltpu.VMEM) for i in range(len(args))]
    out_specs = [pl.BlockSpec(memory_space=pltpu.VMEM)] * len(out_shapes)
    for i in any_outs:
        out_specs[i] = pl.BlockSpec(memory_space=pl.ANY)
    for i, o in aliases.items():
        in_specs[i] = out_specs[o] = pl.BlockSpec(memory_space=pl.ANY)
    return pl.pallas_call(
        kernel,
        out_shape=out_shapes,
        in_specs=in_specs,
        out_specs=out_specs,
        input_output_aliases=aliases,
        scratch_shapes=scratch,
        compiler_params=pltpu.CompilerParams(vmem_limit_bytes=vmem << 20),
        cost_estimate=pl.CostEstimate(flops=flops, bytes_accessed=moved, transcendentals=0),
    )(*args)


def exchange(parts, axis, size, partners):
    return [lax.ppermute(parts[k], axis, [(i, i ^ k) for i in range(size)]) for k in partners]


def gather_space(block, kept, size):
    if size > 8:
        blocks = lax.all_gather(block, "space", axis=0, tiled=True)
        half = blocks.shape[0] // 2
        return [blocks[:half]], [blocks[half:]]
    blocks = [kept, *exchange([block] * size, "space", size, range(size - 2, 0, -2))]
    twins = [twin for b in blocks for twin in exchange([b, b], "space", size, (1,))]
    return blocks + twins[:2], twins[2:]


def per_device(
    var_tokens, key_query, value_weight, qkv_weight, out_weight, up_weight, down_weight, norm_gain
):
    groups = lax.axis_size("var")
    spaces = lax.axis_size("space")
    n_vars, rows, width = var_tokens.shape
    part = rows // groups
    local = qkv_weight.shape[2]
    partners = [range(groups - 1, 0, -1)] * 3
    if groups == 4:
        partners = (3, 2, 1), (1, 3, 2), (2, 1, 3)

    shape = pltpu.VMEM
    kept = (groups, n_vars, part)
    loaded = call(
        load_kernel,
        [
            shape((*kept, width), bf16),
            shape(value_weight.shape, bf16),
            shape((*kept, LANES), bf16),
            shape((groups, part, LANES), bf16),
        ],
        var_tokens.reshape(n_vars, groups, part, width), key_query.T, value_weight,
        flops=2 * n_vars * rows * width * LANES, hbm=3, any_outs=(0, 1),
        scratch=[
            pltpu.VMEM((*kept, width), bf16),
            pltpu.VMEM((H, width), bf16),
            pltpu.SemaphoreType.DMA((3 + groups,)),
        ],
    )
    sent = []
    for slot in reversed(range(groups)):
        sent += call(
            functools.partial(pool_kernel, slot), [shape((part, width + LANES), bf16)],
            *loaded,
            flops=2 * n_vars * part * width * width,
        )
    got = exchange(sent[::-1], "var", groups, partners[0])
    normed, pooled = call(
        norm_kernel, [shape((part, width), bf16)] * 2, norm_gain.reshape(1, width), *got, sent[-1]
    )
    blocks = [*exchange([normed] * groups, "var", groups, partners[1]), normed]
    q, kv, kept = call(
        qkv_kernel,
        [shape((rows, local), bf16)] + [shape((rows, 2 * local), bf16)] * 2,
        qkv_weight.transpose(1, 0, 2), *blocks,
        flops=6 * rows * width * local,
    )
    ffn = []

    def feed_forward(arrived):
        made = call(
            ffn_kernel, [shape((rows, width), f32), shape(arrived.shape, bf16)],
            up_weight, down_weight, *blocks, arrived,
            flops=4 * rows * width * up_weight.shape[1], aliases={2 + len(blocks): 1},
        )
        ffn.append(made[0])
        return made[1]

    early, late = gather_space(kv, feed_forward(kept), spaces)
    heads = H // groups
    state = call(
        functools.partial(early_kernel, heads), [shape((rows, local), f32)] * 3, q, *early,
        flops=4 * rows * rows * len(early) * local * heads, vmem=32,
    )
    sums = call(
        functools.partial(attend_kernel, heads, groups),
        [shape((part, width), bf16)] * groups,
        q, *ffn, out_weight, *state, *late,
        flops=4 * rows * rows * len(late) * local * heads, vmem=32,
    )
    by_partner = dict(zip([*partners[1], 0], sums))
    got = exchange(by_partner, "var", groups, partners[2])
    (out,) = call(
        add_kernel, [jax.ShapeDtypeStruct((part, width), bf16)], pooled, *got, by_partner[0]
    )
    return out


def solution(mesh):
    placed = (
        P("var", "space", None),
        P(),
        P(),
        P(None, None, "var"),
        P("var", None),
        P(None, "var"),
        P("var", None),
        P(),
    )
    return jax.shard_map(
        per_device, mesh=mesh, in_specs=placed, out_specs=P(("space", "var"), None), check_vma=False
    )
```

```python
import functools
import math

import jax
import jax.numpy as jnp
from jax import lax
from jax.experimental import pallas as pl
from jax.experimental.pallas import tpu as pltpu
from jax.sharding import PartitionSpec as P

H = 16
LANES = 128
EPS = 1e-05
f32 = jnp.float32
bf16 = jnp.bfloat16


def rows_of(refs):
    return below([r[...] for r in refs])


def head_spread(first, last, width):
    lane = lax.broadcasted_iota(jnp.int32, (LANES, width), 0)
    column = lax.broadcasted_iota(jnp.int32, (LANES, width), 1)
    group = lane // H
    hit = (lane % H == column // (width // H)) & (group >= first) & (group < last)
    return hit.astype(bf16)


def split3(x):
    hi = x.astype(bf16).astype(f32)
    mid = (x - hi).astype(bf16).astype(f32)
    return hi, mid, x - hi - mid


def below(blocks):
    if blocks[0].shape[0] % 16 == 0:
        return jnp.concatenate(blocks, axis=0)
    return jnp.concatenate([b.astype(f32) for b in blocks], axis=0).astype(bf16)


def load_kernel(x_hbm, kq_hbm, wv_hbm, tokens_any, wv_any, share_ref, stats_ref, x_ref, kq_ref, sem):
    me = lax.axis_index("var")
    slots, n_vars, rows, _ = x_ref.shape
    copies = [pltpu.make_async_copy(kq_hbm, kq_ref, sem.at[0])]
    for k in range(slots):
        copies.append(pltpu.make_async_copy(x_hbm.at[:, me ^ k], x_ref.at[k], sem.at[3 + k]))
    weights = pltpu.make_async_copy(wv_hbm, wv_any, sem.at[1])
    for copy in (*copies, weights):
        copy.start()
    for copy in copies:
        copy.wait()
    passing = pltpu.make_async_copy(x_ref, tokens_any, sem.at[2])
    passing.start()
    x = below([x_ref[k, v] for k in range(slots) for v in range(n_vars)])
    kq = jnp.concatenate([kq_ref[...]] * (LANES // H), axis=0)
    scores = lax.dot_general(x, kq, (((1,), (1,)), ((), ())), preferred_element_type=f32)
    scores = scores.reshape(slots, n_vars, rows, LANES)
    top = jnp.max(scores, axis=1)
    terms = jnp.exp(scores - top[:, None])
    total = jnp.sum(terms, axis=1)
    share_ref[...] = (terms / total[:, None]).astype(bf16)
    lane = lax.broadcasted_iota(jnp.int32, top.shape, 2) // H
    stats = jnp.zeros(top.shape, f32)
    for j, part in enumerate(split3(top) + split3(total)):
        stats = jnp.where(lane == j, part, stats)
    stats_ref[...] = stats.astype(bf16)
    passing.wait()
    weights.wait()


def pool_kernel(slot, x_ref, wv_ref, share_ref, stats_ref, out_ref):
    n_vars, rows, width = x_ref.shape[1:]
    share = below([share_ref[slot, v] for v in range(n_vars)])
    share = jnp.dot(share, head_spread(0, 1, width), preferred_element_type=f32)
    x = below([x_ref[slot, v] for v in range(n_vars)])
    values = jnp.dot(x, wv_ref[...], preferred_element_type=f32)
    mean = jnp.sum((share * values).reshape(n_vars, rows, width), axis=0)
    out_ref[:, :width] = mean.astype(bf16)
    out_ref[:, width:] = stats_ref[slot]


def norm_kernel(gain_ref, *refs):
    parts, (normed_ref, pooled_ref) = refs[:-2], refs[-2:]
    rows, width = normed_ref.shape
    to_top = head_spread(0, 3, width)
    to_total = head_spread(3, 6, width)
    tops = [jnp.dot(p[:, width:], to_top, preferred_element_type=f32) for p in parts]
    totals = [jnp.dot(p[:, width:], to_total, preferred_element_type=f32) for p in parts]
    top = functools.reduce(jnp.maximum, tops)
    scales = [t * jnp.exp(m - top) for t, m in zip(totals, tops)]
    summed = functools.reduce(
        jnp.add, [s * p[:, :width].astype(f32) for s, p in zip(scales, parts)]
    )
    pooled = (summed / functools.reduce(jnp.add, scales)).astype(bf16)
    pooled_ref[...] = pooled
    pooled = pooled.astype(f32)
    centered = pooled - jnp.mean(pooled, axis=1, keepdims=True)
    spread = jnp.mean(centered * centered, axis=1, keepdims=True)
    normed_ref[...] = (centered * lax.rsqrt(spread + EPS) * gain_ref[...].astype(f32)).astype(bf16)


def key_value_kernel(w_ref, *refs):
    blocks, kv_ref = refs[:-1], refs[-1]
    x = rows_of(blocks)
    width = w_ref.shape[2]
    kv_ref[:, :width] = jnp.dot(x, w_ref[1], preferred_element_type=f32).astype(bf16)
    kv_ref[:, width:] = jnp.dot(x, w_ref[2], preferred_element_type=f32).astype(bf16)


def ffn_kernel(up_ref, down_ref, w_ref, kv_ref, *refs):
    blocks, (out_ref, q_ref, kept_ref) = refs[:-3], refs[-3:]
    kept_ref[...] = kv_ref[...]
    x = rows_of(blocks)
    q_ref[...] = jnp.dot(x, w_ref[0], preferred_element_type=f32).astype(bf16)
    hidden = jnp.dot(x, up_ref[...], preferred_element_type=f32)
    hidden = jax.nn.gelu(hidden, approximate=True).astype(bf16)
    out_ref[...] = jnp.dot(hidden, down_ref[...], preferred_element_type=f32)


def attend(heads, q_ref, blocks, span):
    rows, width = q_ref.shape
    head_dim = width // heads
    span = min(width, span)
    owner = lax.broadcasted_iota(jnp.int32, (rows, span), 1) // head_dim
    together = span // head_dim
    results = []
    for first in range(0, width, span):
        own = slice(first, first + span)
        q = q_ref[:, own].astype(f32) * head_dim ** (-0.5)
        q = jnp.concatenate([jnp.where(owner == h, q, 0.0) for h in range(together)], axis=0)
        keys = jnp.concatenate([b[:, own] for b in blocks], axis=0)
        vals = jnp.concatenate([b[:, width + first : width + first + span] for b in blocks], axis=0)
        logits = lax.dot_general(
            q.astype(bf16), keys, (((1,), (1,)), ((), ())), preferred_element_type=f32
        )
        top = jnp.max(logits, axis=1, keepdims=True)
        terms = jnp.exp(logits - top)
        total = jnp.sum(terms, axis=1, keepdims=True)
        mixed = jnp.dot(terms.astype(bf16), vals, preferred_element_type=f32)
        for i, stack in enumerate((mixed, top, total)):
            out = jnp.broadcast_to(stack[:rows], (rows, span))
            for h in range(1, together):
                out = jnp.where(owner == h, stack[h * rows : (h + 1) * rows], out)
            results.append(out)
    return [jnp.concatenate(results[i::3], axis=1) for i in range(3)]


def early_kernel(heads, q_ref, *refs):
    blocks, out_refs = refs[:-3], refs[-3:]
    for ref, value in zip(out_refs, attend(heads, q_ref, blocks, LANES)):
        ref[...] = value


def attend_kernel(heads, groups, q_ref, ffn_ref, wo_ref, mixed_ref, top_ref, total_ref, *refs):
    blocks, out_refs = refs[:-groups], refs[-groups:]
    mixed, top, total = attend(heads, q_ref, blocks, q_ref.shape[1])
    both = jnp.maximum(top, top_ref[...])
    late, early = jnp.exp(top - both), jnp.exp(top_ref[...] - both)
    attended = (mixed * late + mixed_ref[...] * early) / (total * late + total_ref[...] * early)
    out = jnp.dot(attended.astype(bf16), wo_ref[...], preferred_element_type=f32) + ffn_ref[...]
    part = out.shape[0] // groups
    for k in range(groups):
        out_refs[k][...] = out[k * part : (k + 1) * part].astype(bf16)


def add_kernel(*refs):
    out_ref = refs[-1]
    out_ref[...] = functools.reduce(jnp.add, [r[...].astype(f32) for r in refs[:-1]]).astype(bf16)


def call(kernel, out_shapes, *args, flops=0, vmem=16, hbm=0, scratch=(), any_outs=(), aliases={}):
    moved = sum(math.prod(a.shape) * jnp.dtype(a.dtype).itemsize for a in (*args, *out_shapes))
    args = [
        pltpu.with_memory_space_constraint(a, pltpu.HBM if i < hbm else pltpu.VMEM)
        for i, a in enumerate(args)
    ]
    in_specs = [pl.BlockSpec(memory_space=pltpu.HBM if i < hbm else pltpu.VMEM) for i in range(len(args))]
    out_specs = [pl.BlockSpec(memory_space=pltpu.VMEM)] * len(out_shapes)
    for i in any_outs:
        out_specs[i] = pl.BlockSpec(memory_space=pl.ANY)
    for i, o in aliases.items():
        in_specs[i] = out_specs[o] = pl.BlockSpec(memory_space=pl.ANY)
    return pl.pallas_call(
        kernel,
        out_shape=out_shapes,
        in_specs=in_specs,
        out_specs=out_specs,
        input_output_aliases=aliases,
        scratch_shapes=scratch,
        compiler_params=pltpu.CompilerParams(vmem_limit_bytes=vmem << 20),
        cost_estimate=pl.CostEstimate(flops=flops, bytes_accessed=moved, transcendentals=0),
    )(*args)


def exchange(parts, axis, size, partners):
    return [lax.ppermute(parts[k], axis, [(i, i ^ k) for i in range(size)]) for k in partners]


def gather_space(block, kept, size):
    if size > 8:
        blocks = lax.all_gather(block, "space", axis=0, tiled=True)
        half = blocks.shape[0] // 2
        return [blocks[:half]], [blocks[half:]]
    blocks = [kept, *exchange([block] * size, "space", size, range(size - 2, 0, -2))]
    twins = [twin for b in blocks for twin in exchange([b, b], "space", size, (1,))]
    return blocks + twins[:2], twins[2:]


def per_device(
    var_tokens, key_query, value_weight, qkv_weight, out_weight, up_weight, down_weight, norm_gain
):
    groups = lax.axis_size("var")
    spaces = lax.axis_size("space")
    n_vars, rows, width = var_tokens.shape
    part = rows // groups
    local = qkv_weight.shape[2]
    partners = [range(groups - 1, 0, -1)] * 3
    if groups == 4:
        partners = (3, 2, 1), (1, 3, 2), (2, 1, 3)

    shape = pltpu.VMEM
    kept = (groups, n_vars, part)
    loaded = call(
        load_kernel,
        [
            shape((*kept, width), bf16),
            shape(value_weight.shape, bf16),
            shape((*kept, LANES), bf16),
            shape((groups, part, LANES), bf16),
        ],
        var_tokens.reshape(n_vars, groups, part, width), key_query.T, value_weight,
        flops=2 * n_vars * rows * width * LANES, hbm=3, any_outs=(0, 1),
        scratch=[
            pltpu.VMEM((*kept, width), bf16),
            pltpu.VMEM((H, width), bf16),
            pltpu.SemaphoreType.DMA((3 + groups,)),
        ],
    )
    sent = []
    for slot in reversed(range(groups)):
        sent += call(
            functools.partial(pool_kernel, slot), [shape((part, width + LANES), bf16)],
            *loaded,
            flops=2 * n_vars * part * width * width,
        )
    got = exchange(sent[::-1], "var", groups, partners[0])
    normed, pooled = call(
        norm_kernel, [shape((part, width), bf16)] * 2, norm_gain.reshape(1, width), *got, sent[-1]
    )
    blocks = [*exchange([normed] * groups, "var", groups, partners[1]), normed]
    weights = qkv_weight.transpose(1, 0, 2)
    (kv,) = call(
        key_value_kernel, [shape((rows, 2 * local), bf16)], weights, *blocks,
        flops=4 * rows * width * local,
    )
    ffn, q, kept = call(
        ffn_kernel,
        [shape((rows, width), f32), shape((rows, local), bf16), shape(kv.shape, bf16)],
        up_weight, down_weight, weights, kv, *blocks,
        flops=2 * rows * width * (2 * up_weight.shape[1] + local),
    )
    early, late = gather_space(kv, kept, spaces)
    heads = H // groups
    state = call(
        functools.partial(early_kernel, heads), [shape((rows, local), f32)] * 3, q, *early,
        flops=4 * rows * rows * len(early) * local * heads, vmem=32,
    )
    sums = call(
        functools.partial(attend_kernel, heads, groups),
        [shape((part, width), bf16)] * groups,
        q, ffn, out_weight, *state, *late,
        flops=4 * rows * rows * len(late) * local * heads, vmem=32,
    )
    by_partner = dict(zip([*partners[1], 0], sums))
    got = exchange(by_partner, "var", groups, partners[2])
    (out,) = call(
        add_kernel, [jax.ShapeDtypeStruct((part, width), bf16)], pooled, *got, by_partner[0]
    )
    return out


def solution(mesh):
    placed = (
        P("var", "space", None),
        P(),
        P(),
        P(None, None, "var"),
        P("var", None),
        P(None, "var"),
        P("var", None),
        P(),
    )
    return jax.shard_map(
        per_device, mesh=mesh, in_specs=placed, out_specs=P(("space", "var"), None), check_vma=False
    )
```

```python
import functools
import math

import jax
import jax.numpy as jnp
from jax import lax
from jax.experimental import pallas as pl
from jax.experimental.pallas import tpu as pltpu
from jax.sharding import PartitionSpec as P

H = 16
LANES = 128
EPS = 1e-05
f32 = jnp.float32
bf16 = jnp.bfloat16


def rows_of(refs):
    return below([r[...] for r in refs])


def head_spread(first, last, width):
    lane = lax.broadcasted_iota(jnp.int32, (LANES, width), 0)
    column = lax.broadcasted_iota(jnp.int32, (LANES, width), 1)
    group = lane // H
    hit = (lane % H == column // (width // H)) & (group >= first) & (group < last)
    return hit.astype(bf16)


def split3(x):
    hi = x.astype(bf16).astype(f32)
    mid = (x - hi).astype(bf16).astype(f32)
    return hi, mid, x - hi - mid


def below(blocks):
    if blocks[0].shape[0] % 16 == 0:
        return jnp.concatenate(blocks, axis=0)
    return jnp.concatenate([b.astype(f32) for b in blocks], axis=0).astype(bf16)


def load_kernel(x_hbm, kq_hbm, wv_hbm, tokens_any, wv_any, share_ref, stats_ref, x_ref, kq_ref, sem):
    me = lax.axis_index("var")
    slots, n_vars, rows, _ = x_ref.shape
    copies = [pltpu.make_async_copy(kq_hbm, kq_ref, sem.at[0])]
    for k in range(slots):
        copies.append(pltpu.make_async_copy(x_hbm.at[:, me ^ k], x_ref.at[k], sem.at[3 + k]))
    weights = pltpu.make_async_copy(wv_hbm, wv_any, sem.at[1])
    for copy in (*copies, weights):
        copy.start()
    for copy in copies:
        copy.wait()
    passing = pltpu.make_async_copy(x_ref, tokens_any, sem.at[2])
    passing.start()
    x = below([x_ref[k, v] for k in range(slots) for v in range(n_vars)])
    kq = jnp.concatenate([kq_ref[...]] * (LANES // H), axis=0)
    scores = lax.dot_general(x, kq, (((1,), (1,)), ((), ())), preferred_element_type=f32)
    scores = scores.reshape(slots, n_vars, rows, LANES)
    top = jnp.max(scores, axis=1)
    terms = jnp.exp(scores - top[:, None])
    total = jnp.sum(terms, axis=1)
    share_ref[...] = (terms / total[:, None]).astype(bf16)
    lane = lax.broadcasted_iota(jnp.int32, top.shape, 2) // H
    stats = jnp.zeros(top.shape, f32)
    for j, part in enumerate(split3(top) + split3(total)):
        stats = jnp.where(lane == j, part, stats)
    stats_ref[...] = stats.astype(bf16)
    passing.wait()
    weights.wait()


def pool_kernel(slot, x_ref, wv_ref, share_ref, stats_ref, out_ref):
    n_vars, rows, width = x_ref.shape[1:]
    share = below([share_ref[slot, v] for v in range(n_vars)])
    share = jnp.dot(share, head_spread(0, 1, width), preferred_element_type=f32)
    x = below([x_ref[slot, v] for v in range(n_vars)])
    values = jnp.dot(x, wv_ref[...], preferred_element_type=f32)
    mean = jnp.sum((share * values).reshape(n_vars, rows, width), axis=0)
    out_ref[:, :width] = mean.astype(bf16)
    out_ref[:, width:] = stats_ref[slot]


def norm_kernel(gain_ref, *refs):
    parts, (normed_ref, pooled_ref) = refs[:-2], refs[-2:]
    rows, width = normed_ref.shape
    to_top = head_spread(0, 3, width)
    to_total = head_spread(3, 6, width)
    tops = [jnp.dot(p[:, width:], to_top, preferred_element_type=f32) for p in parts]
    totals = [jnp.dot(p[:, width:], to_total, preferred_element_type=f32) for p in parts]
    top = functools.reduce(jnp.maximum, tops)
    scales = [t * jnp.exp(m - top) for t, m in zip(totals, tops)]
    summed = functools.reduce(
        jnp.add, [s * p[:, :width].astype(f32) for s, p in zip(scales, parts)]
    )
    pooled = (summed / functools.reduce(jnp.add, scales)).astype(bf16)
    pooled_ref[...] = pooled
    pooled = pooled.astype(f32)
    centered = pooled - jnp.mean(pooled, axis=1, keepdims=True)
    spread = jnp.mean(centered * centered, axis=1, keepdims=True)
    normed_ref[...] = (centered * lax.rsqrt(spread + EPS) * gain_ref[...].astype(f32)).astype(bf16)


def qkv_kernel(order, w_ref, *refs):
    blocks, (q_ref, kv_ref, kept_ref) = refs[:-3], refs[-3:]
    x = rows_of([blocks[i] for i in order])
    width = q_ref.shape[1]
    q_ref[...] = jnp.dot(x, w_ref[0], preferred_element_type=f32).astype(bf16)
    kv_ref[:, :width] = jnp.dot(x, w_ref[1], preferred_element_type=f32).astype(bf16)
    kv_ref[:, width:] = jnp.dot(x, w_ref[2], preferred_element_type=f32).astype(bf16)
    kept_ref[...] = kv_ref[...]


def ffn_kernel(order, up_ref, down_ref, *refs):
    blocks, out_ref = refs[:-3], refs[-2]
    x = rows_of([blocks[i] for i in order])
    hidden = jnp.dot(x, up_ref[...], preferred_element_type=f32)
    hidden = jax.nn.gelu(hidden, approximate=True).astype(bf16)
    out_ref[...] = jnp.dot(hidden, down_ref[...], preferred_element_type=f32)


def attend(heads, q, blocks):
    rows, width = q.shape
    head_dim = width // heads
    q = q.astype(f32) * head_dim ** (-0.5)
    owner = lax.broadcasted_iota(jnp.int32, (rows, width), 1) // head_dim
    stacked = jnp.concatenate([jnp.where(owner == h, q, 0.0) for h in range(heads)], axis=0)
    stacked = stacked.astype(bf16)
    keys = jnp.concatenate([b[:, :width] for b in blocks], axis=0)
    vals = jnp.concatenate([b[:, width:] for b in blocks], axis=0)
    logits = lax.dot_general(stacked, keys, (((1,), (1,)), ((), ())), preferred_element_type=f32)
    top = jnp.max(logits, axis=1, keepdims=True)
    terms = jnp.exp(logits - top)
    total = jnp.sum(terms, axis=1, keepdims=True)
    mixed = jnp.dot(terms.astype(bf16), vals, preferred_element_type=f32)

    def own_head(stack):
        out = jnp.broadcast_to(stack[:rows], (rows, width))
        for h in range(1, heads):
            out = jnp.where(owner == h, stack[h * rows : (h + 1) * rows], out)
        return out

    return own_head(mixed), own_head(top), own_head(total)


def early_kernel(heads, q_ref, *refs):
    blocks, out_refs = refs[:-3], refs[-3:]
    for ref, value in zip(out_refs, attend(heads, q_ref[...], blocks)):
        ref[...] = value


def attend_kernel(heads, slots, q_ref, ffn_ref, wo_ref, mixed_ref, top_ref, total_ref, *refs):
    n = len(slots)
    blocks, out_refs = refs[:-n], refs[-n:]
    part = out_refs[0].shape[0]
    own = slice(slots[0] * part, (slots[-1] + 1) * part)
    mixed, top, total = attend(heads, q_ref[own], blocks)
    both = jnp.maximum(top, top_ref[own])
    late, early = jnp.exp(top - both), jnp.exp(top_ref[own] - both)
    attended = (mixed * late + mixed_ref[own] * early) / (total * late + total_ref[own] * early)
    out = jnp.dot(attended.astype(bf16), wo_ref[...], preferred_element_type=f32) + ffn_ref[own]
    for i, out_ref in enumerate(out_refs):
        out_ref[...] = out[i * part : (i + 1) * part].astype(bf16)


def add_kernel(*refs):
    out_ref = refs[-1]
    out_ref[...] = functools.reduce(jnp.add, [r[...].astype(f32) for r in refs[:-1]]).astype(bf16)


def call(kernel, out_shapes, *args, flops=0, vmem=16, hbm=0, scratch=(), any_outs=(), aliases={}):
    moved = sum(math.prod(a.shape) * jnp.dtype(a.dtype).itemsize for a in (*args, *out_shapes))
    args = [
        pltpu.with_memory_space_constraint(a, pltpu.HBM if i < hbm else pltpu.VMEM)
        for i, a in enumerate(args)
    ]
    in_specs = [pl.BlockSpec(memory_space=pltpu.HBM if i < hbm else pltpu.VMEM) for i in range(len(args))]
    out_specs = [pl.BlockSpec(memory_space=pltpu.VMEM)] * len(out_shapes)
    for i in any_outs:
        out_specs[i] = pl.BlockSpec(memory_space=pl.ANY)
    for i, o in aliases.items():
        in_specs[i] = out_specs[o] = pl.BlockSpec(memory_space=pl.ANY)
    return pl.pallas_call(
        kernel,
        out_shape=out_shapes,
        in_specs=in_specs,
        out_specs=out_specs,
        input_output_aliases=aliases,
        scratch_shapes=scratch,
        compiler_params=pltpu.CompilerParams(vmem_limit_bytes=vmem << 20),
        cost_estimate=pl.CostEstimate(flops=flops, bytes_accessed=moved, transcendentals=0),
    )(*args)


def exchange(parts, axis, size, partners):
    return [lax.ppermute(parts[k], axis, [(i, i ^ k) for i in range(size)]) for k in partners]


def gather_space(block, kept, size):
    if size > 8:
        blocks = lax.all_gather(block, "space", axis=0, tiled=True)
        half = blocks.shape[0] // 2
        return [blocks[:half]], [blocks[half:]]
    blocks = [kept, *exchange([block] * size, "space", size, range(size - 2, 0, -2))]
    twins = [twin for b in blocks for twin in exchange([b, b], "space", size, (1,))]
    return blocks + twins[:2], twins[2:]


def per_device(
    var_tokens, key_query, value_weight, qkv_weight, out_weight, up_weight, down_weight, norm_gain
):
    groups = lax.axis_size("var")
    spaces = lax.axis_size("space")
    n_vars, rows, width = var_tokens.shape
    part = rows // groups
    local = qkv_weight.shape[2]
    partners = [range(groups - 1, 0, -1)] * 3
    if groups == 4:
        partners = (3, 2, 1), (1, 3, 2), (2, 1, 3)

    shape = pltpu.VMEM
    kept = (groups, n_vars, part)
    loaded = call(
        load_kernel,
        [
            shape((*kept, width), bf16),
            shape(value_weight.shape, bf16),
            shape((*kept, LANES), bf16),
            shape((groups, part, LANES), bf16),
        ],
        var_tokens.reshape(n_vars, groups, part, width), key_query.T, value_weight,
        flops=2 * n_vars * rows * width * LANES, hbm=3, any_outs=(0, 1),
        scratch=[
            pltpu.VMEM((*kept, width), bf16),
            pltpu.VMEM((H, width), bf16),
            pltpu.SemaphoreType.DMA((3 + groups,)),
        ],
    )
    sent = []
    for slot in reversed(range(groups)):
        sent += call(
            functools.partial(pool_kernel, slot), [shape((part, width + LANES), bf16)],
            *loaded,
            flops=2 * n_vars * part * width * width,
        )
    got = exchange(sent[::-1], "var", groups, partners[0])
    normed, pooled = call(
        norm_kernel, [shape((part, width), bf16)] * 2, norm_gain.reshape(1, width), *got, sent[-1]
    )
    blocks = [*exchange([normed] * groups, "var", groups, partners[1]), normed]
    order = [[*partners[1], 0].index(k) for k in (*partners[2], 0)]
    q, kv, kept = call(
        functools.partial(qkv_kernel, order),
        [shape((rows, local), bf16)] + [shape((rows, 2 * local), bf16)] * 2,
        qkv_weight.transpose(1, 0, 2), *blocks,
        flops=6 * rows * width * local,
    )
    ffn = []

    def feed_forward(arrived):
        made = call(
            functools.partial(ffn_kernel, order),
            [shape((rows, width), f32), shape(arrived.shape, bf16)],
            up_weight, down_weight, *blocks, arrived,
            flops=4 * rows * width * up_weight.shape[1], aliases={2 + len(blocks): 1},
        )
        ffn.append(made[0])
        return made[1]

    early, late = gather_space(kv, feed_forward(kept), spaces)
    heads = H // groups
    state = call(
        functools.partial(early_kernel, heads), [shape((rows, local), f32)] * 3, q, *early,
        flops=4 * rows * rows * len(early) * local * heads, vmem=32,
    )
    sums = []
    for slots in (range(groups // 2, groups), range(groups // 2)):
        sums += call(
            functools.partial(attend_kernel, heads, slots),
            [shape((part, width), bf16)] * len(slots),
            q, *ffn, out_weight, *state, *late,
            flops=4 * part * len(slots) * sum(b.shape[0] for b in late) * local * heads, vmem=32,
        )
    rows_of_slots = [*partners[2], 0]
    made_first = rows_of_slots[groups // 2 :]
    by_partner = dict(zip(made_first + rows_of_slots[: groups // 2], sums))
    got = exchange(by_partner, "var", groups, partners[2])
    (out,) = call(
        add_kernel, [jax.ShapeDtypeStruct((part, width), bf16)], pooled, *got, by_partner[0]
    )
    return out


def solution(mesh):
    placed = (
        P("var", "space", None),
        P(),
        P(),
        P(None, None, "var"),
        P("var", None),
        P(None, "var"),
        P("var", None),
        P(),
    )
    return jax.shard_map(
        per_device, mesh=mesh, in_specs=placed, out_specs=P(("space", "var"), None), check_vma=False
    )
```

```python
import functools
import math

import jax
import jax.numpy as jnp
from jax import lax
from jax.experimental import pallas as pl
from jax.experimental.pallas import tpu as pltpu
from jax.sharding import PartitionSpec as P

H = 16
LANES = 128
EPS = 1e-05
f32 = jnp.float32
bf16 = jnp.bfloat16


def rows_of(refs):
    return below([r[...] for r in refs])


def head_spread(first, last, width):
    lane = lax.broadcasted_iota(jnp.int32, (LANES, width), 0)
    column = lax.broadcasted_iota(jnp.int32, (LANES, width), 1)
    group = lane // H
    hit = (lane % H == column // (width // H)) & (group >= first) & (group < last)
    return hit.astype(bf16)


def split3(x):
    hi = x.astype(bf16).astype(f32)
    mid = (x - hi).astype(bf16).astype(f32)
    return hi, mid, x - hi - mid


def below(blocks):
    if blocks[0].shape[0] % 16 == 0:
        return jnp.concatenate(blocks, axis=0)
    return jnp.concatenate([b.astype(f32) for b in blocks], axis=0).astype(bf16)


def load_kernel(x_hbm, kq_hbm, wv_hbm, tokens_any, wv_any, share_ref, stats_ref, x_ref, kq_ref, sem):
    me = lax.axis_index("var")
    slots, n_vars, rows, _ = x_ref.shape
    copies = [pltpu.make_async_copy(kq_hbm, kq_ref, sem.at[0])]
    for k in range(slots):
        copies.append(pltpu.make_async_copy(x_hbm.at[:, me ^ k], x_ref.at[k], sem.at[3 + k]))
    weights = pltpu.make_async_copy(wv_hbm, wv_any, sem.at[1])
    for copy in (*copies, weights):
        copy.start()
    for copy in copies:
        copy.wait()
    passing = pltpu.make_async_copy(x_ref, tokens_any, sem.at[2])
    passing.start()
    x = below([x_ref[k, v] for k in range(slots) for v in range(n_vars)])
    kq = jnp.concatenate([kq_ref[...]] * (LANES // H), axis=0)
    scores = lax.dot_general(x, kq, (((1,), (1,)), ((), ())), preferred_element_type=f32)
    scores = scores.reshape(slots, n_vars, rows, LANES)
    top = jnp.max(scores, axis=1)
    terms = jnp.exp(scores - top[:, None])
    total = jnp.sum(terms, axis=1)
    share_ref[...] = (terms / total[:, None]).astype(bf16)
    lane = lax.broadcasted_iota(jnp.int32, top.shape, 2) // H
    stats = jnp.zeros(top.shape, f32)
    for j, part in enumerate(split3(top) + split3(total)):
        stats = jnp.where(lane == j, part, stats)
    stats_ref[...] = stats.astype(bf16)
    passing.wait()
    weights.wait()


def pool_kernel(slot, x_ref, wv_ref, share_ref, stats_ref, out_ref):
    n_vars, rows, width = x_ref.shape[1:]
    share = below([share_ref[slot, v] for v in range(n_vars)])
    share = jnp.dot(share, head_spread(0, 1, width), preferred_element_type=f32)
    x = below([x_ref[slot, v] for v in range(n_vars)])
    values = jnp.dot(x, wv_ref[...], preferred_element_type=f32)
    mean = jnp.sum((share * values).reshape(n_vars, rows, width), axis=0)
    out_ref[:, :width] = mean.astype(bf16)
    out_ref[:, width:] = stats_ref[slot]


def norm_kernel(gain_ref, *refs):
    parts, (normed_ref, pooled_ref) = refs[:-2], refs[-2:]
    rows, width = normed_ref.shape
    to_top = head_spread(0, 3, width)
    to_total = head_spread(3, 6, width)
    tops = [jnp.dot(p[:, width:], to_top, preferred_element_type=f32) for p in parts]
    totals = [jnp.dot(p[:, width:], to_total, preferred_element_type=f32) for p in parts]
    top = functools.reduce(jnp.maximum, tops)
    scales = [t * jnp.exp(m - top) for t, m in zip(totals, tops)]
    summed = functools.reduce(
        jnp.add, [s * p[:, :width].astype(f32) for s, p in zip(scales, parts)]
    )
    pooled = (summed / functools.reduce(jnp.add, scales)).astype(bf16)
    pooled_ref[...] = pooled
    pooled = pooled.astype(f32)
    centered = pooled - jnp.mean(pooled, axis=1, keepdims=True)
    spread = jnp.mean(centered * centered, axis=1, keepdims=True)
    normed_ref[...] = (centered * lax.rsqrt(spread + EPS) * gain_ref[...].astype(f32)).astype(bf16)


def qkv_kernel(w_ref, *refs):
    blocks, (q_ref, kv_ref, kept_ref) = refs[:-3], refs[-3:]
    x = rows_of(blocks)
    width = q_ref.shape[1]
    q_ref[...] = jnp.dot(x, w_ref[0], preferred_element_type=f32).astype(bf16)
    kv_ref[:, :width] = jnp.dot(x, w_ref[1], preferred_element_type=f32).astype(bf16)
    kv_ref[:, width:] = jnp.dot(x, w_ref[2], preferred_element_type=f32).astype(bf16)
    kept_ref[...] = kv_ref[...]


def ffn_kernel(up_ref, down_ref, *refs):
    blocks, out_ref = refs[:-3], refs[-2]
    x = rows_of(blocks)
    hidden = jnp.dot(x, up_ref[...], preferred_element_type=f32)
    hidden = jax.nn.gelu(hidden, approximate=True).astype(bf16)
    out_ref[...] = jnp.dot(hidden, down_ref[...], preferred_element_type=f32)


def attend(heads, q_ref, blocks):
    rows, width = q_ref.shape
    head_dim = width // heads
    q = q_ref[...].astype(f32) * head_dim ** (-0.5)
    owner = lax.broadcasted_iota(jnp.int32, (rows, width), 1) // head_dim
    stacked = jnp.concatenate([jnp.where(owner == h, q, 0.0) for h in range(heads)], axis=0)
    stacked = stacked.astype(bf16)
    keys = jnp.concatenate([b[:, :width] for b in blocks], axis=0)
    vals = jnp.concatenate([b[:, width:] for b in blocks], axis=0)
    logits = lax.dot_general(stacked, keys, (((1,), (1,)), ((), ())), preferred_element_type=f32)
    top = jnp.max(logits, axis=1, keepdims=True)
    terms = jnp.exp(logits - top)
    total = jnp.sum(terms, axis=1, keepdims=True)
    mixed = jnp.dot(terms.astype(bf16), vals, preferred_element_type=f32)

    def own_head(stack):
        out = jnp.broadcast_to(stack[:rows], (rows, width))
        for h in range(1, heads):
            out = jnp.where(owner == h, stack[h * rows : (h + 1) * rows], out)
        return out

    return own_head(mixed), own_head(top), own_head(total)


def early_kernel(heads, q_ref, *refs):
    blocks, out_refs = refs[:-3], refs[-3:]
    for ref, value in zip(out_refs, attend(heads, q_ref, blocks)):
        ref[...] = value


def attend_kernel(heads, groups, q_ref, ffn_ref, wo_ref, mixed_ref, top_ref, total_ref, *refs):
    blocks, out_refs = refs[:-groups], refs[-groups:]
    mixed, top, total = attend(heads, q_ref, blocks)
    both = jnp.maximum(top, top_ref[...])
    late, early = jnp.exp(top - both), jnp.exp(top_ref[...] - both)
    attended = (mixed * late + mixed_ref[...] * early) / (total * late + total_ref[...] * early)
    out = jnp.dot(attended.astype(bf16), wo_ref[...], preferred_element_type=f32) + ffn_ref[...]
    part = out.shape[0] // groups
    for k in range(groups):
        out_refs[k][...] = out[k * part : (k + 1) * part].astype(bf16)


def add_kernel(*refs):
    out_ref = refs[-1]
    out_ref[...] = functools.reduce(jnp.add, [r[...].astype(f32) for r in refs[:-1]]).astype(bf16)


def call(kernel, out_shapes, *args, flops=0, vmem=16, hbm=0, scratch=(), any_outs=(), aliases={}):
    moved = sum(math.prod(a.shape) * jnp.dtype(a.dtype).itemsize for a in (*args, *out_shapes))
    args = [
        pltpu.with_memory_space_constraint(a, pltpu.HBM if i < hbm else pltpu.VMEM)
        for i, a in enumerate(args)
    ]
    in_specs = [pl.BlockSpec(memory_space=pltpu.HBM if i < hbm else pltpu.VMEM) for i in range(len(args))]
    out_specs = [pl.BlockSpec(memory_space=pltpu.VMEM)] * len(out_shapes)
    for i in any_outs:
        out_specs[i] = pl.BlockSpec(memory_space=pl.ANY)
    for i, o in aliases.items():
        in_specs[i] = out_specs[o] = pl.BlockSpec(memory_space=pl.ANY)
    return pl.pallas_call(
        kernel,
        out_shape=out_shapes,
        in_specs=in_specs,
        out_specs=out_specs,
        input_output_aliases=aliases,
        scratch_shapes=scratch,
        compiler_params=pltpu.CompilerParams(vmem_limit_bytes=vmem << 20),
        cost_estimate=pl.CostEstimate(flops=flops, bytes_accessed=moved, transcendentals=0),
    )(*args)


def exchange(parts, axis, size, partners):
    return [lax.ppermute(parts[k], axis, [(i, i ^ k) for i in range(size)]) for k in partners]


def gather_space(block, kept, size):
    if size > 8:
        blocks = lax.all_gather(block, "space", axis=0, tiled=True)
        half = blocks.shape[0] // 2
        return [blocks[:half]], [blocks[half:]]
    blocks = [kept, *exchange([block] * size, "space", size, (size - 2, *range(2, size - 2, 2)))]
    twins = [twin for b in blocks for twin in exchange([b, b], "space", size, (1,))]
    return blocks + twins[:2], twins[2:]


def per_device(
    var_tokens, key_query, value_weight, qkv_weight, out_weight, up_weight, down_weight, norm_gain
):
    groups = lax.axis_size("var")
    spaces = lax.axis_size("space")
    n_vars, rows, width = var_tokens.shape
    part = rows // groups
    local = qkv_weight.shape[2]
    partners = [range(groups - 1, 0, -1)] * 3
    if groups == 4:
        partners = (3, 2, 1), (1, 3, 2), (2, 1, 3)

    shape = pltpu.VMEM
    kept = (groups, n_vars, part)
    loaded = call(
        load_kernel,
        [
            shape((*kept, width), bf16),
            shape(value_weight.shape, bf16),
            shape((*kept, LANES), bf16),
            shape((groups, part, LANES), bf16),
        ],
        var_tokens.reshape(n_vars, groups, part, width), key_query.T, value_weight,
        flops=2 * n_vars * rows * width * LANES, hbm=3, any_outs=(0, 1),
        scratch=[
            pltpu.VMEM((*kept, width), bf16),
            pltpu.VMEM((H, width), bf16),
            pltpu.SemaphoreType.DMA((3 + groups,)),
        ],
    )
    sent = []
    for slot in reversed(range(groups)):
        sent += call(
            functools.partial(pool_kernel, slot), [shape((part, width + LANES), bf16)],
            *loaded,
            flops=2 * n_vars * part * width * width,
        )
    got = exchange(sent[::-1], "var", groups, partners[0])
    normed, pooled = call(
        norm_kernel, [shape((part, width), bf16)] * 2, norm_gain.reshape(1, width), *got, sent[-1]
    )
    blocks = [*exchange([normed] * groups, "var", groups, partners[1]), normed]
    q, kv, kept = call(
        qkv_kernel,
        [shape((rows, local), bf16)] + [shape((rows, 2 * local), bf16)] * 2,
        qkv_weight.transpose(1, 0, 2), *blocks,
        flops=6 * rows * width * local,
    )
    ffn = []

    def feed_forward(arrived):
        made = call(
            ffn_kernel, [shape((rows, width), f32), shape(arrived.shape, bf16)],
            up_weight, down_weight, *blocks, arrived,
            flops=4 * rows * width * up_weight.shape[1], aliases={2 + len(blocks): 1},
        )
        ffn.append(made[0])
        return made[1]

    early, late = gather_space(kv, feed_forward(kept), spaces)
    heads = H // groups
    state = call(
        functools.partial(early_kernel, heads), [shape((rows, local), f32)] * 3, q, *early,
        flops=4 * rows * rows * len(early) * local * heads, vmem=32,
    )
    sums = call(
        functools.partial(attend_kernel, heads, groups),
        [shape((part, width), bf16)] * groups,
        q, *ffn, out_weight, *state, *late,
        flops=4 * rows * rows * len(late) * local * heads, vmem=32,
    )
    by_partner = dict(zip([*partners[1], 0], sums))
    got = exchange(by_partner, "var", groups, partners[2])
    (out,) = call(
        add_kernel, [jax.ShapeDtypeStruct((part, width), bf16)], pooled, *got, by_partner[0]
    )
    return out


def solution(mesh):
    placed = (
        P("var", "space", None),
        P(),
        P(),
        P(None, None, "var"),
        P("var", None),
        P(None, "var"),
        P("var", None),
        P(),
    )
    return jax.shard_map(
        per_device, mesh=mesh, in_specs=placed, out_specs=P(("space", "var"), None), check_vma=False
    )
```
